32 devices in a mesh: grp: 16 (over z, y, core), dev: 2 (over x).
Axes of the slice: x: 2, y: 2, z: 4, core: 2. Of those that a mesh axis runs over, the one named last changes fastest.
Arguments:
- operators: bfloat16 [64, 1024, 1024], P(('grp', 'dev')), may hold values from -0.3 to 2.3, as said below
- forces: float32 [64, 32, 512], P(('grp', 'dev')), may hold values from -48 to 48
- weights: float32 [64, 512], P(('grp', 'dev')), may hold values from 0.5 to 2
- lengths: int32 [64], replicated, may hold values from 128 to 512, as said below
- slot_order: int32 [64, 512], P(('grp', 'dev')), may hold values from 0 to 511, as said below
Outputs:
- solution: float32 [64, 32, 512], P(('grp', 'dev'))
- residual: float32 [64, 32, 512], P(('grp', 'dev'))
The draws below stay inside these ranges and needn't reach their ends.
Inputs may be any that keep to these rules, and one draw needn't show every extreme that they name: `lengths`: every interface has at least 128 live multipliers and some interface has exactly 512; the last entry belongs to the end of the chain and is not used. `slot_order`: row k is a permutation of 0 to 511 that maps the first lengths[k] positions onto the first lengths[k] slots and leaves the other positions in place. `operators`: each operator is symmetric, and positive definite on every subset of its rows and columns.
All inputs are finite; a program needn't handle non-finite values.
Results may differ from the reference program's by a relative error of at most 0.01.
Values may be sent and summed in bfloat16 or wider, within the bound.
A program may use at most 64 MiB of HBM per device.

```python
import math
import jax
import jax.numpy as jnp
from jax import lax

IFACE = 512
LOADS = 32
ITERS = 2
NSUB = 64


def plan_lengths(key):
    first_key, second_key, third_key, fourth_key = jax.random.split(jax.random.fold_in(key, 17), 4)
    heavy = jax.random.randint(first_key, (NSUB,), 0, 4) == 0
    longer = jax.random.randint(second_key, (NSUB,), IFACE // 2 + 1, IFACE + 1)
    shorter = jax.random.randint(third_key, (NSUB,), IFACE // 4, IFACE // 2 + 1)
    drawn = jnp.where(heavy, longer, shorter).astype(jnp.int32)
    chosen = jax.random.randint(fourth_key, (), 0, max(NSUB - 1, 1))
    return drawn.at[chosen].set(IFACE).astype(jnp.int32)


def draw_lengths(key, part):
    return plan_lengths(key)


def draw_slot_order(key, part):
    drawn = plan_lengths(key)
    many_keys = jax.random.split(jax.random.fold_in(key, 29), NSUB)
    rankings = jax.vmap(lambda sub_key: jax.random.permutation(sub_key, IFACE))(many_keys).astype(jnp.int32)
    positions = jnp.arange(IFACE, dtype=jnp.int32)
    scores = jnp.where(positions[None, :] < drawn[:, None], rankings, IFACE + positions[None, :])
    return jnp.argsort(scores, axis=1, stable=True).astype(jnp.int32)


def draw_operators(key, part):
    extent = 2 * IFACE
    spread = 0.35 / math.sqrt(extent)

    def single(subdomain):
        sub_key = jax.random.fold_in(jax.random.fold_in(key, 41), subdomain)
        first_key, second_key = jax.random.split(sub_key)
        noise = jax.random.normal(first_key, (extent, extent), jnp.float32) * spread
        symmetric = (noise + noise.T) / math.sqrt(2.0)
        diagonal = jax.random.uniform(second_key, (extent,), jnp.float32, 1.0, 2.0)
        return (symmetric + jnp.diag(diagonal)).astype(jnp.bfloat16)
    return lax.map(single, jnp.arange(NSUB))


def draw_forces(key, part):
    first_key = jax.random.fold_in(jax.random.fold_in(key, 53), 0)
    growth = 3.0 ** (jnp.arange(NSUB, dtype=jnp.float32) / max(NSUB - 1, 1))
    noise = jnp.clip(jax.random.normal(first_key, (NSUB, LOADS, IFACE), jnp.float32), -6.0, 6.0)
    return noise * growth[:, None, None]


def steps_of(rng, shape, pieces, smallest, top_value):
    gain = 1.0
    for position, blocks in pieces:
        heights = jax.random.uniform(jax.random.fold_in(jax.random.fold_in(rng, 6), position), (blocks,), jnp.float32, smallest / len(pieces), top_value / len(pieces))
        gain = gain * jnp.repeat(jnp.exp(heights), shape[position] // blocks).reshape((-1,) + (1,) * (len(shape) - 1 - position))
    return gain


def setup_inputs(seed: int = 0) -> dict:
    keys = jax.random.split(jax.random.key(seed), 6)
    return {
        "operators": draw_operators(jax.random.fold_in(keys[5], 71), 0),
        "forces": draw_forces(jax.random.fold_in(keys[5], 71), 0),
        "weights": jnp.clip(jnp.exp(math.log(2.0) - 1.3862944 * jax.random.uniform(keys[2], (NSUB, IFACE), jnp.float32) ** steps_of(keys[2], (NSUB, IFACE), ((0, 32),), -0.2, 0.2)), 0.5, 2.0),
        "lengths": draw_lengths(jax.random.fold_in(keys[5], 71), 0),
        "slot_order": draw_slot_order(jax.random.fold_in(keys[5], 71), 0),
    }


def cholesky_solve(matrix, target):
    factor = jnp.linalg.cholesky(matrix)
    halfway = lax.linalg.triangular_solve(factor, target, left_side=True, lower=True)
    return lax.linalg.triangular_solve(factor, halfway, left_side=True, lower=True, transpose_a=True)

def inner(first, second):
    return jnp.einsum('kri,kti->rt', first, second, precision=lax.Precision.HIGHEST)

def combine(field, matrix):
    return jnp.einsum('kri,rt->kti', field, matrix, precision=lax.Precision.HIGHEST)

def reference(operators, forces, weights, lengths, slot_order):
    breadth = forces.shape[2]
    chain = jnp.arange(NSUB, dtype=jnp.int32)
    effective = jnp.where(chain < NSUB - 1, lengths, 0)
    positions = jnp.arange(breadth, dtype=jnp.int32)
    live_mask = (positions[None, :] < effective[:, None]).astype(jnp.float32)[:, None, :]
    inverse = jnp.argsort(slot_order, axis=1).astype(jnp.int32)

    def operate(field):
        turned = jnp.take_along_axis(field, slot_order[:, None, :], axis=2)
        left_input = jnp.concatenate([jnp.zeros_like(turned[:1]), turned[:-1]], axis=0)
        inputs = jnp.concatenate([left_input, field], axis=2).astype(jnp.bfloat16)

        def single(pair):
            return jnp.dot(pair[0].astype(jnp.float32), pair[1].astype(jnp.float32), preferred_element_type=jnp.float32)
        products = lax.map(single, (inputs, operators))
        left_part = products[:, :, :breadth]
        right_part = products[:, :, breadth:]
        returned = jnp.concatenate([left_part[1:], jnp.zeros_like(left_part[:1])], axis=0)
        return live_mask * (right_part + jnp.take_along_axis(returned, inverse[:, None, :], axis=2))
    residual = live_mask * forces
    solution = jnp.zeros_like(residual)
    search = weights[:, None, :] * residual
    for iteration in range(ITERS):
        image = operate(search)
        curvature = inner(search, image)
        projection = inner(search, residual)
        alpha = cholesky_solve(curvature, projection)
        solution = solution + combine(search, alpha)
        residual = residual - combine(image, alpha)
        if iteration + 1 < ITERS:
            scaled = weights[:, None, :] * residual
            cross = inner(image, scaled)
            beta = -cholesky_solve(curvature, cross)
            search = scaled + combine(search, beta)
    return (solution, residual)
```

```python
import functools

import jax
import jax.numpy as jnp
from jax import lax
from jax.experimental import pallas as pl
from jax.experimental.pallas import tpu as pltpu
from jax.sharding import PartitionSpec as P

MESH = pl.DeviceIdType.MESH
F32, BF16 = jnp.float32, jnp.bfloat16
EXACT = lax.Precision.HIGHEST


def plan_stages(groups, devs):
    factors = []
    while groups > 1:
        factor = next((f for f in (4, 3, 2, 5, 7) if groups % f == 0), groups)
        factors.append(factor)
        groups //= factor
    first = factors[0] if factors else 1
    stages, stride = [(devs * first, None, first)], first
    for factor in factors[1:]:
        stages.append((factor, stride, factor))
        stride *= factor
    return [stage for stage in stages if stage[0] > 1]


def peer(stage, offset, grp, dev, devs):
    size, stride, factor = stage
    if stride is None:
        low = lax.rem(grp, factor)
        place = lax.rem(low * devs + dev + offset, size)
        return grp - low + lax.div(place, devs), lax.rem(place, devs)
    digit = lax.rem(lax.div(grp, stride), factor)
    return grp + (lax.rem(digit + offset, factor) - digit) * stride, dev


def split(x):
    high = x.astype(BF16)
    return high, (x - high.astype(F32)).astype(BF16)


def dot(x, y):
    return jnp.dot(x, y, preferred_element_type=F32)


def dot_nt(x, y, precision=None):
    return lax.dot_general(
        x, y, (((1,), (1,)), ((), ())), precision=precision, preferred_element_type=F32
    )


def small(x, y):
    return jnp.dot(x, y, precision=EXACT, preferred_element_type=F32)


def small_tn(x, y):
    return lax.dot_general(
        x, y, (((0,), (0,)), ((), ())), precision=EXACT, preferred_element_type=F32
    )


def pack(matrix):
    size = matrix.shape[0]
    parts = max(1, min(128 // size, size // 8))
    rows = size // parts
    return jnp.concatenate([matrix[i * rows : (i + 1) * rows] for i in range(parts)], axis=1)


def unpack(packed, size):
    parts = packed.shape[1] // size
    return jnp.concatenate([packed[:, i * size : (i + 1) * size] for i in range(parts)], axis=0)


def eliminate(matrix, targets):
    size = matrix.shape[0]
    held = jnp.concatenate([matrix, targets], axis=1)
    rows = lax.broadcasted_iota(jnp.int32, (size, 1), 0)
    for p in range(size):
        row = held[p : p + 1, :]
        row = row / row[:, p : p + 1]
        held = jnp.where(rows == p, row, held - held[:, p : p + 1] * row)
    return held[:, size:]


def kernel(stages, devs, total, lengths_ref, forces_ref, weights_ref, order_ref, operators_ref,
           solution_ref, residual_ref,
           ops, pick, start, search, image, remainder, scaled, second, product,
           fwd_src, fwd_dst, fwd2_src, fwd2_dst, ret_src, ret_dst, retlow_src, retlow_dst,
           ret2_src, ret2_dst, sums_src, sums_dst, last_src, last_dst,
           ops_sem, halo_send, halo_recv, sums_send, sums_recv, last_send, last_recv):
    number, loads, breadth = forces_ref.shape
    grp, dev = lax.axis_index("grp"), lax.axis_index("dev")
    me = grp * devs + dev
    has_prev, has_next = me > 0, me < total - 1
    before, after = jnp.maximum(me - 1, 0), jnp.minimum(me + 1, total - 1)
    prev_id = (lax.div(before, devs), lax.rem(before, devs))
    next_id = (lax.div(after, devs), lax.rem(after, devs))

    barrier = pltpu.get_barrier_semaphore()
    partners = 0
    for stage in stages:
        for offset in range(1, stage[0]):
            pl.semaphore_signal(barrier, inc=1, device_id=peer(stage, offset, grp, dev, devs), device_id_type=MESH)
            partners += 1

    @pl.when(has_prev)
    def _():
        pl.semaphore_signal(barrier, inc=1, device_id=prev_id, device_id_type=MESH)

    @pl.when(has_next)
    def _():
        pl.semaphore_signal(barrier, inc=1, device_id=next_id, device_id_type=MESH)

    loading = [pltpu.make_async_copy(operators_ref.at[l], ops.at[l], ops_sem.at[l]) for l in range(number)]
    for copy in loading:
        copy.start()

    def remote(slot, source, target, where):
        return pltpu.make_async_remote_copy(
            src_ref=source, dst_ref=target, send_sem=halo_send.at[slot], recv_sem=halo_recv.at[slot],
            device_id=where, device_id_type=MESH,
        )

    forward = remote(0, fwd_src.at[0], fwd_dst.at[0], next_id)
    forward_low = remote(1, fwd_src.at[1], fwd_dst.at[1], next_id)
    forward_second = remote(2, fwd2_src, fwd2_dst, next_id)
    back = remote(3, ret_src, ret_dst, prev_id)
    back_low = remote(4, retlow_src, retlow_dst, prev_id)
    back_second = remote(5, ret2_src, ret2_dst, prev_id)

    def start_if(condition, *copies):
        @pl.when(condition)
        def _():
            for copy in copies:
                copy.start()

    def arrived(condition, copy, buffer):
        @pl.when(condition)
        def _():
            copy.wait_recv()

        @pl.when(jnp.logical_not(condition))
        def _():
            buffer[...] = jnp.zeros_like(buffer)

    positions = lax.broadcasted_iota(jnp.int32, (1, breadth), 1)
    masks = []
    for l in range(number):
        k = me * number + l
        live = jnp.where(k < total * number - 1, lengths_ref[k], 0)
        masks.append(positions < live)
    slots = lax.broadcasted_iota(jnp.int32, (breadth, breadth), 0)

    turned = [None] * number
    stacks = [None] * number
    for l in reversed(range(number)):
        pick[l] = jnp.where(slots == order_ref[l : l + 1, :], 1.0, 0.0).astype(BF16)
        start[l] = jnp.where(masks[l], forces_ref[l], 0.0)
        search[l] = start[l] * weights_ref[l : l + 1, :]
        high, low = split(search[l])
        stacks[l] = jnp.concatenate([high, low], axis=0)
        turned[l] = dot(stacks[l], pick[l]).astype(BF16)
        if l == number - 1:
            fwd_src[0] = turned[l][:loads]
            fwd_src[1] = turned[l][loads:]
            pl.semaphore_wait(barrier, partners + has_prev.astype(jnp.int32) + has_next.astype(jnp.int32))
            start_if(has_next, forward, forward_low)

    for copy in loading:
        copy.wait()

    def own_products(stacks, turned):
        product[0] = dot(stacks[0], ops[0, breadth:, :])
        for l in range(1, number):
            product[l] = dot(jnp.concatenate([turned[l - 1], stacks[l]], axis=1), ops[l])

    def gather(l, field):
        high, low = split(field)
        both = dot_nt(jnp.concatenate([high, low], axis=0), pick[l])
        return both[:loads] + both[loads:]

    own_products(stacks, turned)
    arrived(has_prev, forward, fwd_dst.at[0])
    product[0, :loads, :] += dot(fwd_dst[0], ops[0, :breadth, :])
    ret_src[...] = product[0, :loads, :breadth]
    start_if(has_prev, back)
    arrived(has_prev, forward_low, fwd_dst.at[1])
    product[0, loads:, :] += dot(fwd_dst[1], ops[0, :breadth, :])
    retlow_src[...] = product[0, loads:, :breadth].astype(BF16)
    start_if(has_prev, back_low)

    def finish_image(l, left):
        image[l] = jnp.where(masks[l], product[l, :loads, breadth:] + gather(l, left), 0.0)
        scaled[l] = weights_ref[l : l + 1, :] * image[l]
        high, low = split(scaled[l])
        stacks[l] = jnp.concatenate([high, low], axis=0)
        turned[l] = dot(stacks[l], pick[l]).astype(BF16)

    for l in range(number):
        remainder[l] = product[l, loads:, breadth:]
        if l < number - 1:
            finish_image(l, product[l + 1, :loads, :breadth])
            remainder[l] += dot_nt(product[l + 1, loads:, :breadth].astype(BF16), pick[l])
    arrived(has_next, back, ret_dst)
    finish_image(number - 1, ret_dst[...])
    fwd2_src[...] = turned[number - 1]
    start_if(has_next, forward_second)

    def exchange(s, source, inbox, send_sem, recv_sem):
        copies = []
        for offset in range(1, stages[s][0]):
            place = sum(stage[0] - 1 for stage in stages[:s]) + offset - 1
            copies.append(pltpu.make_async_remote_copy(
                src_ref=source.at[s], dst_ref=inbox.at[place], send_sem=send_sem.at[place],
                recv_sem=recv_sem.at[place], device_id=peer(stages[s], offset, grp, dev, devs),
                device_id_type=MESH,
            ))
            copies[-1].start()
        return copies

    def collect(s, copies, source, inbox):
        first = sum(stage[0] - 1 for stage in stages[:s])
        value = source[s]
        for i, copy in enumerate(copies):
            copy.wait_recv()
            value = value + inbox[first + i]
        return value

    curvature = projection = middle = 0.0
    for l in range(number):
        pair = dot_nt(jnp.concatenate([search[l], scaled[l]], axis=0), image[l], EXACT)
        curvature, middle = curvature + pair[:loads], middle + pair[loads:]
        projection = projection + dot_nt(search[l], start[l], EXACT)
    tall = pack(curvature).shape[0]
    sums_src[0] = jnp.concatenate([pack(curvature), pack(projection), pack(middle)], axis=0)
    pending = [exchange(0, sums_src, sums_dst, sums_send, sums_recv)]

    own_products(stacks, turned)

    def energy(pair, values):
        return dot_nt(pair[:loads].astype(F32) + pair[loads:].astype(F32), values[:loads] + values[loads:], EXACT)

    outer = 0.0
    for l in range(number):
        outer = outer + energy(stacks[l], product[l, :, breadth:])
        if l > 0:
            outer = outer + energy(turned[l - 1], product[l, :, :breadth])
    arrived(has_prev, forward_second, fwd2_dst)
    extra = dot(fwd2_dst[...], ops[0, :breadth, :])
    product[0] += extra
    ret2_src[...] = product[0, :loads, :breadth] + product[0, loads:, :breadth]
    start_if(has_prev, back_second)
    outer = outer + energy(stacks[0], extra[:, breadth:]) + energy(fwd2_dst[...], product[0, :, :breadth])
    last_src[0] = pack(outer)
    trailing = [exchange(0, last_src, last_dst, last_send, last_recv)]

    for s in range(1, len(stages)):
        sums_src[s] = collect(s - 1, pending[-1], sums_src, sums_dst)
        pending.append(exchange(s, sums_src, sums_dst, sums_send, sums_recv))
        last_src[s] = collect(s - 1, trailing[-1], last_src, last_dst)
        trailing.append(exchange(s, last_src, last_dst, last_send, last_recv))

    for l in range(number):
        right = product[l, :loads, breadth:] + product[l, loads:, breadth:]
        if l < number - 1:
            left = product[l + 1, :loads, :breadth] + product[l + 1, loads:, :breadth]
        else:
            arrived(has_next, back_low, retlow_dst)
            remainder[l] += dot_nt(retlow_dst[...], pick[l])
            arrived(has_next, back_second, ret2_dst)
            left = ret2_dst[...]
        remainder[l] = jnp.where(masks[l], remainder[l], 0.0)
        second[l] = jnp.where(masks[l], right + gather(l, left), 0.0)

    summed = collect(len(stages) - 1, pending[-1], sums_src, sums_dst)
    curvature = unpack(summed[:tall], loads)
    projection = unpack(summed[tall : 2 * tall], loads)
    middle = unpack(summed[2 * tall :], loads)
    solved = eliminate(curvature, jnp.concatenate([projection, middle], axis=1))
    alpha = solved[:, :loads]
    shift = small(solved[:, loads:], alpha)
    right_side = small_tn(alpha, small(middle, alpha) - curvature)
    known = small(middle, shift)
    outer = unpack(collect(len(stages) - 1, trailing[-1], last_src, last_dst), loads)
    again = small_tn(alpha, small(outer, alpha) - known)
    alpha2 = eliminate(again, right_side)
    shifted = small(shift, alpha2)
    onward = small(alpha, alpha2)
    total_alpha = alpha + shifted
    for l in range(number):
        solution_ref[l] = small_tn(
            jnp.concatenate([total_alpha, -onward], axis=0), jnp.concatenate([search[l], scaled[l]], axis=0)
        )
        residual_ref[l] = start[l] - small_tn(
            jnp.concatenate([total_alpha, shifted, -onward], axis=0),
            jnp.concatenate([image[l], remainder[l], second[l]], axis=0),
        )

    @pl.when(has_next)
    def _():
        for copy in (forward, forward_low, forward_second):
            copy.wait_send()

    @pl.when(has_prev)
    def _():
        for copy in (back, back_low, back_second):
            copy.wait_send()

    for copies in pending + trailing:
        for copy in copies:
            copy.wait_send()


def body(stages, devs, total, operators, forces, weights, lengths, slot_order):
    number, loads, breadth = forces.shape
    tall, wide = jax.eval_shape(pack, jax.ShapeDtypeStruct((loads, loads), F32)).shape
    boxes = sum(stage[0] - 1 for stage in stages)
    field = pltpu.VMEM(forces.shape, F32)
    vmem = pl.BlockSpec(memory_space=pltpu.VMEM)
    return tuple(pl.pallas_call(
        functools.partial(kernel, stages, devs, total),
        out_shape=[jax.ShapeDtypeStruct(forces.shape, F32)] * 2,
        in_specs=[pl.BlockSpec(memory_space=pltpu.SMEM), vmem, vmem, vmem, pl.BlockSpec(memory_space=pl.ANY)],
        out_specs=[vmem, vmem],
        scratch_shapes=[
            pltpu.VMEM(operators.shape, BF16),
            pltpu.VMEM((number, breadth, breadth), BF16),
            field, field, field, field, field, field,
            pltpu.VMEM((number, 2 * loads, 2 * breadth), F32),
            pltpu.VMEM((2, loads, breadth), BF16),
            pltpu.VMEM((2, loads, breadth), BF16),
            pltpu.VMEM((2 * loads, breadth), BF16),
            pltpu.VMEM((2 * loads, breadth), BF16),
            pltpu.VMEM((loads, breadth), F32),
            pltpu.VMEM((loads, breadth), F32),
            pltpu.VMEM((loads, breadth), BF16),
            pltpu.VMEM((loads, breadth), BF16),
            pltpu.VMEM((loads, breadth), F32),
            pltpu.VMEM((loads, breadth), F32),
            pltpu.VMEM((len(stages), 3 * tall, wide), F32),
            pltpu.VMEM((boxes, 3 * tall, wide), F32),
            pltpu.VMEM((len(stages), tall, wide), F32),
            pltpu.VMEM((boxes, tall, wide), F32),
            pltpu.SemaphoreType.DMA((number,)),
            pltpu.SemaphoreType.DMA((6,)),
            pltpu.SemaphoreType.DMA((6,)),
            pltpu.SemaphoreType.DMA((boxes,)),
            pltpu.SemaphoreType.DMA((boxes,)),
            pltpu.SemaphoreType.DMA((boxes,)),
            pltpu.SemaphoreType.DMA((boxes,)),
        ],
        compiler_params=pltpu.CompilerParams(
            collective_id=0, has_side_effects=True, vmem_limit_bytes=40 * 1024 * 1024
        ),
        cost_estimate=pl.CostEstimate(
            flops=12 * number * loads * 4 * breadth * breadth,
            bytes_accessed=operators.size * 2 + 4 * forces.size * 4,
            transcendentals=0,
        ),
    )(lengths, forces, weights, slot_order, operators))


def solution(mesh):
    devs, groups = mesh.shape["dev"], mesh.shape["grp"]
    stages = plan_stages(groups, devs)
    in_specs = (
        P(("grp", "dev"), None, None),
        P(("grp", "dev"), None, None),
        P(("grp", "dev"), None),
        P(),
        P(("grp", "dev"), None),
    )
    out_specs = (P(("grp", "dev"), None, None), P(("grp", "dev"), None, None))
    return jax.shard_map(
        functools.partial(body, stages, devs, devs * groups),
        mesh=mesh, in_specs=in_specs, out_specs=out_specs, check_vma=False,
    )
```

```python
import functools

import jax
import jax.numpy as jnp
from jax import lax
from jax.experimental import pallas as pl
from jax.experimental.pallas import tpu as pltpu
from jax.sharding import PartitionSpec as P

MESH = pl.DeviceIdType.MESH
F32, BF16 = jnp.float32, jnp.bfloat16
EXACT = lax.Precision.HIGHEST


def plan_stages(groups, devs):
    factors = []
    while groups > 1:
        factor = next((f for f in (4, 3, 2, 5, 7) if groups % f == 0), groups)
        factors.append(factor)
        groups //= factor
    first = factors[0] if factors else 1
    stages, stride = [(devs * first, None, first)], first
    for factor in factors[1:]:
        stages.append((factor, stride, factor))
        stride *= factor
    return [stage for stage in stages if stage[0] > 1]


def peer(stage, offset, grp, dev, devs):
    size, stride, factor = stage
    if stride is None:
        low = lax.rem(grp, factor)
        place = lax.rem(low * devs + dev + offset, size)
        return grp - low + lax.div(place, devs), lax.rem(place, devs)
    digit = lax.rem(lax.div(grp, stride), factor)
    return grp + (lax.rem(digit + offset, factor) - digit) * stride, dev


def split(x):
    high = x.astype(BF16)
    return high, (x - high.astype(F32)).astype(BF16)


def dot(x, y):
    return jnp.dot(x, y, preferred_element_type=F32)


def dot_nt(x, y, precision=None):
    return lax.dot_general(
        x, y, (((1,), (1,)), ((), ())), precision=precision, preferred_element_type=F32
    )


def small(x, y):
    return jnp.dot(x, y, precision=EXACT, preferred_element_type=F32)


def small_tn(x, y):
    return lax.dot_general(
        x, y, (((0,), (0,)), ((), ())), precision=EXACT, preferred_element_type=F32
    )


def pack(matrix):
    size = matrix.shape[0]
    parts = max(1, min(128 // size, size // 8))
    rows = size // parts
    return jnp.concatenate([matrix[i * rows : (i + 1) * rows] for i in range(parts)], axis=1)


def unpack(packed, size):
    parts = packed.shape[1] // size
    return jnp.concatenate([packed[:, i * size : (i + 1) * size] for i in range(parts)], axis=0)


def eliminate(matrix, targets, between=None):
    size = matrix.shape[0]
    held = jnp.concatenate([matrix, targets], axis=1)
    width = held.shape[1]
    index = lax.broadcasted_iota(jnp.int32, (size, 1), 0)
    block = 4 if size % 4 == 0 else 1
    for p in range(0, size, block):
        if between is not None and p == size // 2:
            between()
        rows = [held[p + i : p + i + 1, :] for i in range(block)]
        entries = [
            [jnp.broadcast_to(row[:, p + j : p + j + 1], (1, width)) for j in range(block)] for row in rows
        ]
        columns = [held[:, p + j : p + j + 1] for j in range(block)]
        for i in range(block):
            scale = 1.0 / entries[i][i]
            rows[i] = rows[i] * scale
            entries[i] = [entry * scale for entry in entries[i]]
            for k in range(block):
                if k != i:
                    factor = entries[k][i]
                    rows[k] = rows[k] - factor * rows[i]
                    entries[k] = [a - factor * b for a, b in zip(entries[k], entries[i])]
        update = columns[0] * rows[0]
        for j in range(1, block):
            update = update + columns[j] * rows[j]
        held = held - update
        for j in range(block):
            held = jnp.where(index == p + j, rows[j], held)
    return held[:, size:]


def kernel(stages, devs, total, lengths_hbm, forces_hbm, weights_hbm, order_hbm, operators_ref,
           solution_ref, residual_ref,
           lengths_ref, forces_ref, weights_ref, order_ref, ops, pick, start, search, image, remainder, scaled, second, product,
           fwd_src, fwd_dst, fwd2_src, fwd2_dst, ret_src, ret_dst, retlow_src, retlow_dst,
           ret2_src, ret2_dst, sums_src, sums_dst, last_src, last_dst,
           ops_sem, small_sem, halo_send, halo_recv, sums_send, sums_recv, last_send, last_recv):
    number, loads, breadth = forces_ref.shape
    grp, dev = lax.axis_index("grp"), lax.axis_index("dev")
    me = grp * devs + dev
    has_prev, has_next = me > 0, me < total - 1
    before, after = jnp.maximum(me - 1, 0), jnp.minimum(me + 1, total - 1)
    prev_id = (lax.div(before, devs), lax.rem(before, devs))
    next_id = (lax.div(after, devs), lax.rem(after, devs))

    barrier = pltpu.get_barrier_semaphore()
    partners = 0
    for stage in stages:
        for offset in range(1, stage[0]):
            pl.semaphore_signal(barrier, inc=1, device_id=peer(stage, offset, grp, dev, devs), device_id_type=MESH)
            partners += 1

    @pl.when(has_prev)
    def _():
        pl.semaphore_signal(barrier, inc=1, device_id=prev_id, device_id_type=MESH)

    @pl.when(has_next)
    def _():
        pl.semaphore_signal(barrier, inc=1, device_id=next_id, device_id_type=MESH)

    fetching = [
        pltpu.make_async_copy(source, target, small_sem.at[i])
        for i, (source, target) in enumerate((
            (order_hbm, order_ref), (forces_hbm, forces_ref), (weights_hbm, weights_ref), (lengths_hbm, lengths_ref),
        ))
    ]
    for copy in fetching:
        copy.start()
    loading = [pltpu.make_async_copy(operators_ref.at[l], ops.at[l], ops_sem.at[l]) for l in range(number)]
    for copy in loading:
        copy.start()

    def remote(slot, source, target, where):
        return pltpu.make_async_remote_copy(
            src_ref=source, dst_ref=target, send_sem=halo_send.at[slot], recv_sem=halo_recv.at[slot],
            device_id=where, device_id_type=MESH,
        )

    forward = remote(0, fwd_src.at[0], fwd_dst.at[0], next_id)
    forward_low = remote(1, fwd_src.at[1], fwd_dst.at[1], next_id)
    forward_second = remote(2, fwd2_src, fwd2_dst, next_id)
    back = remote(3, ret_src, ret_dst, prev_id)
    back_low = remote(4, retlow_src, retlow_dst, prev_id)
    back_second = remote(5, ret2_src, ret2_dst, prev_id)

    def start_if(condition, *copies):
        @pl.when(condition)
        def _():
            for copy in copies:
                copy.start()

    def arrived(condition, copy, buffer):
        @pl.when(condition)
        def _():
            copy.wait_recv()

        @pl.when(jnp.logical_not(condition))
        def _():
            buffer[...] = jnp.zeros_like(buffer)

    for copy in fetching:
        copy.wait()
    positions = lax.broadcasted_iota(jnp.int32, (1, breadth), 1)
    masks = []
    for l in range(number):
        k = me * number + l
        live = jnp.where(k < total * number - 1, lengths_ref[k], 0)
        masks.append(positions < live)
    slots = lax.broadcasted_iota(jnp.int32, (breadth, breadth), 0)

    turned = [None] * number
    stacks = [None] * number
    for l in reversed(range(number)):
        pick[l] = jnp.where(slots == order_ref[l : l + 1, :], 1.0, 0.0).astype(BF16)
        start[l] = jnp.where(masks[l], forces_ref[l], 0.0)
        search[l] = start[l] * weights_ref[l : l + 1, :]
        high, low = split(search[l])
        stacks[l] = jnp.concatenate([high, low], axis=0)
        turned[l] = dot(stacks[l], pick[l]).astype(BF16)
        if l == number - 1:
            fwd_src[0] = turned[l][:loads]
            fwd_src[1] = turned[l][loads:]
            pl.semaphore_wait(barrier, partners + has_prev.astype(jnp.int32) + has_next.astype(jnp.int32))
            start_if(has_next, forward, forward_low)

    for copy in loading:
        copy.wait()

    def own_products(stacks, turned):
        product[0] = dot(stacks[0], ops[0, breadth:, :])
        for l in range(1, number):
            product[l] = dot(jnp.concatenate([turned[l - 1], stacks[l]], axis=1), ops[l])

    def gather(l, field):
        high, low = split(field)
        both = dot_nt(jnp.concatenate([high, low], axis=0), pick[l])
        return both[:loads] + both[loads:]

    own_products(stacks, turned)
    arrived(has_prev, forward, fwd_dst.at[0])
    ret_src[...] = product[0, :loads, :breadth] + dot(fwd_dst[0], ops[0, :breadth, :breadth])
    start_if(has_prev, back)
    product[0, :loads, breadth:] += dot(fwd_dst[0], ops[0, :breadth, breadth:])
    arrived(has_prev, forward_low, fwd_dst.at[1])
    product[0, loads:, :] += dot(fwd_dst[1], ops[0, :breadth, :])
    retlow_src[...] = product[0, loads:, :breadth].astype(BF16)
    start_if(has_prev, back_low)

    def finish_image(l, left):
        image[l] = jnp.where(masks[l], product[l, :loads, breadth:] + gather(l, left), 0.0)
        scaled[l] = weights_ref[l : l + 1, :] * image[l]
        high, low = split(scaled[l])
        stacks[l] = jnp.concatenate([high, low], axis=0)
        turned[l] = dot(stacks[l], pick[l]).astype(BF16)

    def gram(l):
        pair = dot_nt(jnp.concatenate([search[l], scaled[l]], axis=0), image[l], EXACT)
        return pair[:loads], pair[loads:]

    curvature = projection = middle = 0.0
    for l in range(number):
        remainder[l] = product[l, loads:, breadth:]
        projection = projection + dot_nt(search[l], start[l], EXACT)
        if l < number - 1:
            finish_image(l, product[l + 1, :loads, :breadth])
            remainder[l] += dot_nt(product[l + 1, loads:, :breadth].astype(BF16), pick[l])
            first, second_part = gram(l)
            curvature, middle = curvature + first, middle + second_part
    arrived(has_next, back, ret_dst)
    finish_image(number - 1, ret_dst[...])
    fwd2_src[...] = turned[number - 1]
    start_if(has_next, forward_second)
    first, second_part = gram(number - 1)
    curvature, middle = curvature + first, middle + second_part

    def exchange(s, source, inbox, send_sem, recv_sem):
        copies = []
        for offset in range(1, stages[s][0]):
            place = sum(stage[0] - 1 for stage in stages[:s]) + offset - 1
            copies.append(pltpu.make_async_remote_copy(
                src_ref=source.at[s], dst_ref=inbox.at[place], send_sem=send_sem.at[place],
                recv_sem=recv_sem.at[place], device_id=peer(stages[s], offset, grp, dev, devs),
                device_id_type=MESH,
            ))
            copies[-1].start()
        return copies

    def collect(s, copies, source, inbox):
        first = sum(stage[0] - 1 for stage in stages[:s])
        value = source[s]
        for i, copy in enumerate(copies):
            copy.wait_recv()
            value = value + inbox[first + i]
        return value

    tall = pack(curvature).shape[0]
    sums_src[0] = jnp.concatenate([pack(curvature), pack(projection), pack(middle)], axis=0)
    pending = [exchange(0, sums_src, sums_dst, sums_send, sums_recv)]

    own_products(stacks, turned)

    def energy(pair, values):
        return dot_nt(pair[:loads].astype(F32) + pair[loads:].astype(F32), values[:loads] + values[loads:], EXACT)

    outer = 0.0
    for l in range(number):
        outer = outer + energy(stacks[l], product[l, :, breadth:])
        if l > 0:
            outer = outer + energy(turned[l - 1], product[l, :, :breadth])
    for s in range(1, len(stages)):
        sums_src[s] = collect(s - 1, pending[-1], sums_src, sums_dst)
        pending.append(exchange(s, sums_src, sums_dst, sums_send, sums_recv))
    arrived(has_prev, forward_second, fwd2_dst)
    left_own = product[0, :, :breadth]
    left_extra = dot(fwd2_dst[...], ops[0, :breadth, :breadth])
    mixed = energy(fwd2_dst[...], left_extra + 2.0 * left_own)
    outer = outer + mixed
    last_src[0] = pack(outer)
    trailing = [exchange(0, last_src, last_dst, last_send, last_recv)]
    left_total = left_own + left_extra
    ret2_src[...] = left_total[:loads] + left_total[loads:]
    start_if(has_prev, back_second)
    product[0, :, breadth:] += dot(fwd2_dst[...], ops[0, :breadth, breadth:])

    def advance():
        for s in range(1, len(stages)):
            last_src[s] = collect(s - 1, trailing[-1], last_src, last_dst)
            trailing.append(exchange(s, last_src, last_dst, last_send, last_recv))

    summed = collect(len(stages) - 1, pending[-1], sums_src, sums_dst)
    curvature = unpack(summed[:tall], loads)
    projection = unpack(summed[tall : 2 * tall], loads)
    middle = unpack(summed[2 * tall :], loads)
    solved = eliminate(curvature, jnp.concatenate([projection, middle], axis=1), advance)
    alpha = solved[:, :loads]
    shift = small(solved[:, loads:], alpha)
    right_side = small_tn(alpha, small(middle, alpha) - curvature)
    known = small(middle, shift)
    for l in range(number):
        right = product[l, :loads, breadth:] + product[l, loads:, breadth:]
        if l < number - 1:
            left = product[l + 1, :loads, :breadth] + product[l + 1, loads:, :breadth]
        else:
            arrived(has_next, back_low, retlow_dst)
            remainder[l] += dot_nt(retlow_dst[...], pick[l])
            arrived(has_next, back_second, ret2_dst)
            left = ret2_dst[...]
        remainder[l] = jnp.where(masks[l], remainder[l], 0.0)
        second[l] = jnp.where(masks[l], right + gather(l, left), 0.0)

    outer = unpack(collect(len(stages) - 1, trailing[-1], last_src, last_dst), loads)
    outer = 0.5 * (outer + outer.T)
    again = small_tn(alpha, small(outer, alpha) - known)
    alpha2 = eliminate(again, right_side)
    for l in range(number):
        following = small_tn(shift, search[l]) - small_tn(alpha, scaled[l])
        solution_ref[l] = small_tn(alpha, search[l]) + small_tn(alpha2, following)
        moved = small_tn(shift, image[l] + remainder[l]) - small_tn(alpha, second[l])
        residual_ref[l] = start[l] - small_tn(alpha, image[l]) - small_tn(alpha2, moved)

    @pl.when(has_next)
    def _():
        for copy in (forward, forward_low, forward_second):
            copy.wait_send()

    @pl.when(has_prev)
    def _():
        for copy in (back, back_low, back_second):
            copy.wait_send()

    for copies in pending + trailing:
        for copy in copies:
            copy.wait_send()


def body(stages, devs, total, operators, forces, weights, lengths, slot_order):
    number, loads, breadth = forces.shape
    tall, wide = jax.eval_shape(pack, jax.ShapeDtypeStruct((loads, loads), F32)).shape
    boxes = sum(stage[0] - 1 for stage in stages)
    field = pltpu.VMEM(forces.shape, F32)
    vmem = pl.BlockSpec(memory_space=pltpu.VMEM)
    return tuple(pl.pallas_call(
        functools.partial(kernel, stages, devs, total),
        out_shape=[jax.ShapeDtypeStruct(forces.shape, F32)] * 2,
        in_specs=[pl.BlockSpec(memory_space=pl.ANY)] * 5,
        out_specs=[vmem, vmem],
        scratch_shapes=[
            pltpu.SMEM(lengths.shape, jnp.int32),
            field,
            pltpu.VMEM(weights.shape, F32),
            pltpu.VMEM(slot_order.shape, jnp.int32),
            pltpu.VMEM(operators.shape, BF16),
            pltpu.VMEM((number, breadth, breadth), BF16),
            field, field, field, field, field, field,
            pltpu.VMEM((number, 2 * loads, 2 * breadth), F32),
            pltpu.VMEM((2, loads, breadth), BF16),
            pltpu.VMEM((2, loads, breadth), BF16),
            pltpu.VMEM((2 * loads, breadth), BF16),
            pltpu.VMEM((2 * loads, breadth), BF16),
            pltpu.VMEM((loads, breadth), F32),
            pltpu.VMEM((loads, breadth), F32),
            pltpu.VMEM((loads, breadth), BF16),
            pltpu.VMEM((loads, breadth), BF16),
            pltpu.VMEM((loads, breadth), F32),
            pltpu.VMEM((loads, breadth), F32),
            pltpu.VMEM((len(stages), 3 * tall, wide), F32),
            pltpu.VMEM((boxes, 3 * tall, wide), F32),
            pltpu.VMEM((len(stages), tall, wide), F32),
            pltpu.VMEM((boxes, tall, wide), F32),
            pltpu.SemaphoreType.DMA((number,)),
            pltpu.SemaphoreType.DMA((4,)),
            pltpu.SemaphoreType.DMA((6,)),
            pltpu.SemaphoreType.DMA((6,)),
            pltpu.SemaphoreType.DMA((boxes,)),
            pltpu.SemaphoreType.DMA((boxes,)),
            pltpu.SemaphoreType.DMA((boxes,)),
            pltpu.SemaphoreType.DMA((boxes,)),
        ],
        compiler_params=pltpu.CompilerParams(
            collective_id=0, has_side_effects=True, vmem_limit_bytes=60 * 1024 * 1024
        ),
        cost_estimate=pl.CostEstimate(
            flops=12 * number * loads * 4 * breadth * breadth,
            bytes_accessed=operators.size * 2 + 4 * forces.size * 4,
            transcendentals=0,
        ),
    )(lengths, forces, weights, slot_order, operators))


def solution(mesh):
    devs, groups = mesh.shape["dev"], mesh.shape["grp"]
    stages = plan_stages(groups, devs)
    in_specs = (
        P(("grp", "dev"), None, None),
        P(("grp", "dev"), None, None),
        P(("grp", "dev"), None),
        P(),
        P(("grp", "dev"), None),
    )
    out_specs = (P(("grp", "dev"), None, None), P(("grp", "dev"), None, None))
    return jax.shard_map(
        functools.partial(body, stages, devs, devs * groups),
        mesh=mesh, in_specs=in_specs, out_specs=out_specs, check_vma=False,
    )
```

```python
import functools

import jax
import jax.numpy as jnp
from jax import lax
from jax.experimental import pallas as pl
from jax.experimental.pallas import tpu as pltpu
from jax.sharding import PartitionSpec as P

MESH = pl.DeviceIdType.MESH
F32, BF16 = jnp.float32, jnp.bfloat16
VMEM_BYTES = 60 * 1024 * 1024
EXACT = lax.Precision.HIGHEST


def plan_stages(groups, devs):
    factors = []
    while groups > 1:
        factor = next((f for f in (4, 3, 2, 5, 7) if groups % f == 0), groups)
        factors.append(factor)
        groups //= factor
    first = factors[0] if factors else 1
    stages, stride = [(devs * first, None, first)], first
    for factor in factors[1:]:
        stages.append((factor, stride, factor))
        stride *= factor
    return [stage for stage in stages if stage[0] > 1]


def peer(stage, offset, grp, dev, devs):
    size, stride, factor = stage
    if stride is None:
        low = lax.rem(grp, factor)
        place = lax.rem(low * devs + dev + offset, size)
        return grp - low + lax.div(place, devs), lax.rem(place, devs)
    digit = lax.rem(lax.div(grp, stride), factor)
    return grp + (lax.rem(digit + offset, factor) - digit) * stride, dev


def split(x):
    high = x.astype(BF16)
    return high, (x - high.astype(F32)).astype(BF16)


def dot(x, y):
    return jnp.dot(x, y, preferred_element_type=F32)


def dot_nt(x, y, precision=None):
    return lax.dot_general(
        x, y, (((1,), (1,)), ((), ())), precision=precision, preferred_element_type=F32
    )


def small(x, y):
    return jnp.dot(x, y, precision=EXACT, preferred_element_type=F32)


def small_tn(x, y):
    return lax.dot_general(
        x, y, (((0,), (0,)), ((), ())), precision=EXACT, preferred_element_type=F32
    )


def pack(matrix):
    size = matrix.shape[0]
    parts = max(1, min(128 // size, size // 8))
    rows = size // parts
    return jnp.concatenate([matrix[i * rows : (i + 1) * rows] for i in range(parts)], axis=1)


def unpack(packed, size):
    parts = packed.shape[1] // size
    return jnp.concatenate([packed[:, i * size : (i + 1) * size] for i in range(parts)], axis=0)


def eliminate(matrix, targets, between=None):
    size = matrix.shape[0]
    held = jnp.concatenate([matrix, targets], axis=1)
    width = held.shape[1]
    index = lax.broadcasted_iota(jnp.int32, (size, 1), 0)
    block = 4 if size % 4 == 0 else 1
    for p in range(0, size, block):
        if between is not None and p == size // 2:
            between()
        rows = [held[p + i : p + i + 1, :] for i in range(block)]
        entries = [
            [jnp.broadcast_to(row[:, p + j : p + j + 1], (1, width)) for j in range(block)] for row in rows
        ]
        columns = [held[:, p + j : p + j + 1] for j in range(block)]
        for i in range(block):
            scale = 1.0 / entries[i][i]
            rows[i] = rows[i] * scale
            entries[i] = [entry * scale for entry in entries[i]]
            for k in range(block):
                if k != i:
                    factor = entries[k][i]
                    rows[k] = rows[k] - factor * rows[i]
                    entries[k] = [a - factor * b for a, b in zip(entries[k], entries[i])]
        update = columns[0] * rows[0]
        for j in range(1, block):
            update = update + columns[j] * rows[j]
        held = held - update
        for j in range(block):
            held = jnp.where(index == p + j, rows[j], held)
    return held[:, size:]


def kernel(stages, devs, total, lengths_hbm, forces_hbm, weights_hbm, order_hbm, operators_ref,
           solution_ref, residual_ref,
           lengths_ref, forces_ref, weights_ref, order_ref, ops, pick, start, search, image, remainder, scaled, second, product, applied,
           fwd_src, fwd_dst, fwdlow_src, fwdlow_dst, right_src, right_dst, ret_src, ret_dst, retlow_src, retlow_dst,
           ret2_src, ret2_dst, sums_src, sums_dst, last_src, last_dst,
           ops_sem, small_sem, halo_send, halo_recv, sums_send, sums_recv, last_send, last_recv):
    number, loads, breadth = forces_ref.shape
    grp, dev = lax.axis_index("grp"), lax.axis_index("dev")
    me = grp * devs + dev
    has_prev, has_next = me > 0, me < total - 1
    before, after = jnp.maximum(me - 1, 0), jnp.minimum(me + 1, total - 1)
    prev_id = (lax.div(before, devs), lax.rem(before, devs))
    next_id = (lax.div(after, devs), lax.rem(after, devs))

    barrier = pltpu.get_barrier_semaphore()
    partners = 0
    for stage in stages:
        for offset in range(1, stage[0]):
            pl.semaphore_signal(barrier, inc=1, device_id=peer(stage, offset, grp, dev, devs), device_id_type=MESH)
            partners += 1

    @pl.when(has_prev)
    def _():
        pl.semaphore_signal(barrier, inc=1, device_id=prev_id, device_id_type=MESH)

    @pl.when(has_next)
    def _():
        pl.semaphore_signal(barrier, inc=1, device_id=next_id, device_id_type=MESH)

    fetching = [
        pltpu.make_async_copy(source, target, small_sem.at[i])
        for i, (source, target) in enumerate((
            (order_hbm, order_ref), (forces_hbm, forces_ref), (weights_hbm, weights_ref), (lengths_hbm, lengths_ref),
        ))
    ]
    for copy in fetching:
        copy.start()
    loading = [pltpu.make_async_copy(operators_ref.at[l], ops.at[l], ops_sem.at[l]) for l in reversed(range(number))]
    for copy in loading:
        copy.start()

    def remote(slot, source, target, where):
        return pltpu.make_async_remote_copy(
            src_ref=source, dst_ref=target, send_sem=halo_send.at[slot], recv_sem=halo_recv.at[slot],
            device_id=where, device_id_type=MESH,
        )

    forward = remote(0, fwd_src, fwd_dst, next_id)
    forward_low = remote(1, fwdlow_src, fwdlow_dst, next_id)
    forward_right = remote(2, right_src, right_dst, next_id)
    back = remote(3, ret_src, ret_dst, prev_id)
    back_low = remote(4, retlow_src, retlow_dst, prev_id)
    back_second = remote(5, ret2_src, ret2_dst, prev_id)

    def start_if(condition, *copies):
        @pl.when(condition)
        def _():
            for copy in copies:
                copy.start()

    def arrived(condition, copy, buffer):
        @pl.when(condition)
        def _():
            copy.wait_recv()

        @pl.when(jnp.logical_not(condition))
        def _():
            buffer[...] = jnp.zeros_like(buffer)

    for copy in fetching:
        copy.wait()
    positions = lax.broadcasted_iota(jnp.int32, (1, breadth), 1)
    masks = []
    for l in range(number):
        k = me * number + l
        live = jnp.where(k < total * number - 1, lengths_ref[k], 0)
        masks.append(positions < live)
    slots = lax.broadcasted_iota(jnp.int32, (breadth, breadth), 0)

    last = number - 1
    turned = [None] * number
    stacks = [None] * number
    for l in reversed(range(number)):
        pick[l] = jnp.where(slots == order_ref[l : l + 1, :], 1.0, 0.0).astype(BF16)
        start[l] = jnp.where(masks[l], forces_ref[l], 0.0)
        search[l] = start[l] * weights_ref[l : l + 1, :]
        stacks[l] = jnp.concatenate(split(search[l]), axis=0)
        if l == last:
            spread = [jnp.broadcast_to(x, (16, breadth)) for x in split(weights_ref[l : l + 1, :])]
            sent = dot(jnp.concatenate([stacks[l]] + spread, axis=0), pick[l]).astype(BF16)
            fwd_src[...] = sent[:loads]
            fwdlow_src[...] = sent[loads:]
            pl.semaphore_wait(barrier, partners + has_prev.astype(jnp.int32) + has_next.astype(jnp.int32))
            start_if(has_next, forward, forward_low)
        else:
            turned[l] = dot(stacks[l], pick[l]).astype(BF16)

    def gather(l, field):
        both = dot_nt(jnp.concatenate(split(field), axis=0), pick[l])
        return both[:loads] + both[loads:]

    def apply(l, fields, target):
        target[l] = dot(jnp.concatenate(fields, axis=1), ops[l])

    loading[0].wait()
    apply(last, [turned[last - 1], stacks[last]], product)
    both = dot(jnp.concatenate(split(product[last, :loads, breadth:]), axis=0), pick[last])
    right_src[...] = both[:loads] + both[loads:]
    start_if(has_next, forward_right)
    for copy in loading[1:]:
        copy.wait()
    for l in range(1, last):
        apply(l, [turned[l - 1], stacks[l]], product)
    product[0] = dot(stacks[0], ops[0, breadth:, :])
    projection = 0.0
    for l in range(number):
        projection = projection + dot_nt(search[l], start[l], EXACT)

    def finish_image(l, left):
        image[l] = jnp.where(masks[l], product[l, :loads, breadth:] + gather(l, left), 0.0)
        scaled[l] = weights_ref[l : l + 1, :] * image[l]
        stacks[l] = jnp.concatenate(split(scaled[l]), axis=0)

    def gram(direction, along, values):
        pair = dot_nt(jnp.concatenate([direction, along], axis=0), values, EXACT)
        return pair[:loads], pair[loads:]

    arrived(has_prev, forward, fwd_dst)
    owed = product[0, :loads, :breadth] + dot(fwd_dst[...], ops[0, :breadth, :breadth])
    ret_src[...] = owed
    start_if(has_prev, back)
    product[0, :loads, breadth:] += dot(fwd_dst[...], ops[0, :breadth, breadth:])
    curvature = middle = 0.0
    for l in range(last):
        finish_image(l, product[l + 1, :loads, :breadth])
        turned[l] = dot(stacks[l], pick[l]).astype(BF16)
        first, other = gram(search[l], scaled[l], image[l])
        curvature, middle = curvature + first, middle + other

    arrived(has_prev, forward_low, fwdlow_dst)
    arrived(has_prev, forward_right, right_dst)
    incoming = positions < jnp.where(has_prev, lengths_ref[jnp.maximum(me * number - 1, 0)], 0)
    across = jnp.where(incoming, right_dst[...] + owed, 0.0)
    turned_weights = (
        fwdlow_dst[loads : loads + 16].astype(F32) + fwdlow_dst[loads + 16 : loads + 32].astype(F32)
    )[:1]
    across_scaled = turned_weights * across
    across_stack = jnp.concatenate(split(across_scaled), axis=0)
    first, other = gram(
        fwd_dst[...].astype(F32) + fwdlow_dst[:loads].astype(F32), across_scaled, across
    )
    curvature, middle = curvature + first, middle + other

    def exchange(s, source, inbox, send_sem, recv_sem):
        copies = []
        for offset in range(1, stages[s][0]):
            place = sum(stage[0] - 1 for stage in stages[:s]) + offset - 1
            copies.append(pltpu.make_async_remote_copy(
                src_ref=source.at[s], dst_ref=inbox.at[place], send_sem=send_sem.at[place],
                recv_sem=recv_sem.at[place], device_id=peer(stages[s], offset, grp, dev, devs),
                device_id_type=MESH,
            ))
            copies[-1].start()
        return copies

    def collect(s, copies, source, inbox):
        first = sum(stage[0] - 1 for stage in stages[:s])
        value = source[s]
        for i, copy in enumerate(copies):
            copy.wait_recv()
            value = value + inbox[first + i]
        return value

    tall = pack(curvature).shape[0]
    sums_src[0] = jnp.concatenate([pack(curvature), pack(projection), pack(middle)], axis=0)
    pending = [exchange(0, sums_src, sums_dst, sums_send, sums_recv)]

    def energy(pair, values):
        return dot_nt(pair[:loads].astype(F32) + pair[loads:].astype(F32), values[:loads] + values[loads:], EXACT)

    apply(0, [across_stack, stacks[0]], applied)
    ret2_src[...] = applied[0, :loads, :breadth] + applied[0, loads:, :breadth]
    outer = energy(across_stack, applied[0, :, :breadth]) + energy(stacks[0], applied[0, :, breadth:])
    for l in range(1, last):
        apply(l, [turned[l - 1], stacks[l]], applied)
        outer = outer + energy(turned[l - 1], applied[l, :, :breadth]) + energy(stacks[l], applied[l, :, breadth:])
    applied[last] = dot(turned[last - 1], ops[last, :breadth, :])
    outer = outer + energy(turned[last - 1], applied[last, :, :breadth])

    for s in range(1, len(stages)):
        sums_src[s] = collect(s - 1, pending[-1], sums_src, sums_dst)
        pending.append(exchange(s, sums_src, sums_dst, sums_send, sums_recv))

    arrived(has_next, back, ret_dst)
    finish_image(last, ret_dst[...])
    own = dot(stacks[last], ops[last, breadth:, breadth:])
    outer = outer + energy(stacks[last], own + 2.0 * applied[last, :, breadth:])
    last_src[0] = pack(outer)
    trailing = [exchange(0, last_src, last_dst, last_send, last_recv)]
    start_if(has_prev, back_second)

    product[0, loads:, :] += dot(fwdlow_dst[:loads], ops[0, :breadth, :])
    retlow_src[...] = product[0, loads:, :breadth].astype(BF16)
    start_if(has_prev, back_low)
    applied[last, :, breadth:] += own
    applied[last, :, :breadth] += dot(stacks[last], ops[last, breadth:, :breadth])

    def advance():
        for s in range(1, len(stages)):
            last_src[s] = collect(s - 1, trailing[-1], last_src, last_dst)
            trailing.append(exchange(s, last_src, last_dst, last_send, last_recv))

    summed = collect(len(stages) - 1, pending[-1], sums_src, sums_dst)
    curvature = unpack(summed[:tall], loads)
    projection = unpack(summed[tall : 2 * tall], loads)
    middle = unpack(summed[2 * tall :], loads)
    solved = eliminate(curvature, jnp.concatenate([projection, middle], axis=1), advance)
    alpha = solved[:, :loads]
    shift = small(solved[:, loads:], alpha)
    right_side = small_tn(alpha, small(middle, alpha) - curvature)
    known = small(middle, shift)
    for l in range(number):
        right = applied[l, :loads, breadth:] + applied[l, loads:, breadth:]
        if l < last:
            left_low = product[l + 1, loads:, :breadth].astype(BF16)
            left = applied[l + 1, :loads, :breadth] + applied[l + 1, loads:, :breadth]
        else:
            arrived(has_next, back_low, retlow_dst)
            left_low = retlow_dst[...]
            arrived(has_next, back_second, ret2_dst)
            left = ret2_dst[...]
        remainder[l] = jnp.where(masks[l], product[l, loads:, breadth:] + dot_nt(left_low, pick[l]), 0.0)
        second[l] = jnp.where(masks[l], right + gather(l, left), 0.0)
    outer = unpack(collect(len(stages) - 1, trailing[-1], last_src, last_dst), loads)
    outer = 0.5 * (outer + outer.T)
    again = small_tn(alpha, small(outer, alpha) - known)
    alpha2 = eliminate(again, right_side)
    for l in range(number):
        following = small_tn(shift, search[l]) - small_tn(alpha, scaled[l])
        solution_ref[l] = small_tn(alpha, search[l]) + small_tn(alpha2, following)
        moved = small_tn(shift, image[l] + remainder[l]) - small_tn(alpha, second[l])
        residual_ref[l] = start[l] - small_tn(alpha, image[l]) - small_tn(alpha2, moved)

    @pl.when(has_next)
    def _():
        for copy in (forward, forward_low, forward_right):
            copy.wait_send()

    @pl.when(has_prev)
    def _():
        for copy in (back, back_low, back_second):
            copy.wait_send()

    for copies in pending + trailing:
        for copy in copies:
            copy.wait_send()


def hand_over(*fields):
    count, number = len(fields), fields[0].shape[0]

    def copies(*refs):
        sources, targets, sems = refs[:count], refs[count : 2 * count], refs[2 * count]
        moving = [
            pltpu.make_async_copy(sources[i].at[l], targets[i].at[l], sems.at[i * number + l])
            for i in range(count) for l in range(number)
        ]
        for copy in moving:
            copy.start()
        for copy in moving:
            copy.wait()

    anywhere = pl.BlockSpec(memory_space=pl.ANY)
    return tuple(pl.pallas_call(
        copies,
        out_shape=[jax.ShapeDtypeStruct(field.shape, field.dtype) for field in fields],
        in_specs=[anywhere] * count,
        out_specs=[anywhere] * count,
        scratch_shapes=[pltpu.SemaphoreType.DMA((count * number,))],
        compiler_params=pltpu.CompilerParams(vmem_limit_bytes=VMEM_BYTES),
    )(*fields))


def body(stages, devs, total, operators, forces, weights, lengths, slot_order):
    number, loads, breadth = forces.shape
    tall, wide = jax.eval_shape(pack, jax.ShapeDtypeStruct((loads, loads), F32)).shape
    boxes = sum(stage[0] - 1 for stage in stages)
    field = pltpu.VMEM(forces.shape, F32)
    vmem = pl.BlockSpec(memory_space=pltpu.VMEM)
    results = pl.pallas_call(
        functools.partial(kernel, stages, devs, total),
        out_shape=[jax.ShapeDtypeStruct(forces.shape, F32)] * 2,
        in_specs=[pl.BlockSpec(memory_space=pl.ANY)] * 5,
        out_specs=[vmem, vmem],
        scratch_shapes=[
            pltpu.SMEM(lengths.shape, jnp.int32),
            field,
            pltpu.VMEM(weights.shape, F32),
            pltpu.VMEM(slot_order.shape, jnp.int32),
            pltpu.VMEM(operators.shape, BF16),
            pltpu.VMEM((number, breadth, breadth), BF16),
            field, field, field, field, field, field,
            pltpu.VMEM((number, 2 * loads, 2 * breadth), F32),
            pltpu.VMEM((number, 2 * loads, 2 * breadth), F32),
            pltpu.VMEM((loads, breadth), BF16),
            pltpu.VMEM((loads, breadth), BF16),
            pltpu.VMEM((loads + 32, breadth), BF16),
            pltpu.VMEM((loads + 32, breadth), BF16),
            pltpu.VMEM((loads, breadth), F32),
            pltpu.VMEM((loads, breadth), F32),
            pltpu.VMEM((loads, breadth), F32),
            pltpu.VMEM((loads, breadth), F32),
            pltpu.VMEM((loads, breadth), BF16),
            pltpu.VMEM((loads, breadth), BF16),
            pltpu.VMEM((loads, breadth), F32),
            pltpu.VMEM((loads, breadth), F32),
            pltpu.VMEM((len(stages), 3 * tall, wide), F32),
            pltpu.VMEM((boxes, 3 * tall, wide), F32),
            pltpu.VMEM((len(stages), tall, wide), F32),
            pltpu.VMEM((boxes, tall, wide), F32),
            pltpu.SemaphoreType.DMA((number,)),
            pltpu.SemaphoreType.DMA((4,)),
            pltpu.SemaphoreType.DMA((6,)),
            pltpu.SemaphoreType.DMA((6,)),
            pltpu.SemaphoreType.DMA((boxes,)),
            pltpu.SemaphoreType.DMA((boxes,)),
            pltpu.SemaphoreType.DMA((boxes,)),
            pltpu.SemaphoreType.DMA((boxes,)),
        ],
        compiler_params=pltpu.CompilerParams(
            collective_id=0, has_side_effects=True, vmem_limit_bytes=VMEM_BYTES
        ),
        cost_estimate=pl.CostEstimate(
            flops=12 * number * loads * 4 * breadth * breadth,
            bytes_accessed=operators.size * 2 + 4 * forces.size * 4,
            transcendentals=0,
        ),
    )(lengths, forces, weights, slot_order, operators)
    return hand_over(*results)


def solution(mesh):
    devs, groups = mesh.shape["dev"], mesh.shape["grp"]
    stages = plan_stages(groups, devs)
    in_specs = (
        P(("grp", "dev"), None, None),
        P(("grp", "dev"), None, None),
        P(("grp", "dev"), None),
        P(),
        P(("grp", "dev"), None),
    )
    out_specs = (P(("grp", "dev"), None, None), P(("grp", "dev"), None, None))
    return jax.shard_map(
        functools.partial(body, stages, devs, devs * groups),
        mesh=mesh, in_specs=in_specs, out_specs=out_specs, check_vma=False,
    )
```

```python
import functools

import jax
import jax.numpy as jnp
from jax import lax
from jax.experimental import pallas as pl
from jax.experimental.pallas import tpu as pltpu
from jax.sharding import PartitionSpec as P

MESH = pl.DeviceIdType.MESH
F32, BF16 = jnp.float32, jnp.bfloat16
VMEM_BYTES = 60 * 1024 * 1024
EXACT = lax.Precision.HIGHEST


def plan_stages(groups, devs):
    factors = []
    while groups > 1:
        factor = next((f for f in (4, 3, 2, 5, 7) if groups % f == 0), groups)
        factors.append(factor)
        groups //= factor
    first = factors[0] if factors else 1
    stages, stride = [(devs * first, None, first)], first
    for factor in factors[1:]:
        stages.append((factor, stride, factor))
        stride *= factor
    return [stage for stage in stages if stage[0] > 1]


def peer(stage, offset, grp, dev, devs):
    size, stride, factor = stage
    if stride is None:
        low = lax.rem(grp, factor)
        place = lax.rem(low * devs + dev + offset, size)
        return grp - low + lax.div(place, devs), lax.rem(place, devs)
    digit = lax.rem(lax.div(grp, stride), factor)
    return grp + (lax.rem(digit + offset, factor) - digit) * stride, dev


def split(x):
    high = x.astype(BF16)
    return high, (x - high.astype(F32)).astype(BF16)


def dot(x, y):
    return jnp.dot(x, y, preferred_element_type=F32)


def dot_nt(x, y, precision=None):
    return lax.dot_general(
        x, y, (((1,), (1,)), ((), ())), precision=precision, preferred_element_type=F32
    )


def small(x, y):
    return jnp.dot(x, y, precision=EXACT, preferred_element_type=F32)


def small_tn(x, y):
    return lax.dot_general(
        x, y, (((0,), (0,)), ((), ())), precision=EXACT, preferred_element_type=F32
    )


def pack(matrix):
    size = matrix.shape[0]
    parts = max(1, min(128 // size, size // 8))
    rows = size // parts
    return jnp.concatenate([matrix[i * rows : (i + 1) * rows] for i in range(parts)], axis=1)


def unpack(packed, size):
    parts = packed.shape[1] // size
    return jnp.concatenate([packed[:, i * size : (i + 1) * size] for i in range(parts)], axis=0)


def eliminate(matrix, targets, between=None):
    size = matrix.shape[0]
    held = jnp.concatenate([matrix, targets], axis=1)
    width = held.shape[1]
    index = lax.broadcasted_iota(jnp.int32, (size, 1), 0)
    block = 4 if size % 4 == 0 else 1
    for p in range(0, size, block):
        if between is not None and p == size // 2:
            between()
        rows = [held[p + i : p + i + 1, :] for i in range(block)]
        entries = [
            [jnp.broadcast_to(row[:, p + j : p + j + 1], (1, width)) for j in range(block)] for row in rows
        ]
        columns = [held[:, p + j : p + j + 1] for j in range(block)]
        for i in range(block):
            scale = 1.0 / entries[i][i]
            rows[i] = rows[i] * scale
            entries[i] = [entry * scale for entry in entries[i]]
            for k in range(block):
                if k != i:
                    factor = entries[k][i]
                    rows[k] = rows[k] - factor * rows[i]
                    entries[k] = [a - factor * b for a, b in zip(entries[k], entries[i])]
        update = columns[0] * rows[0]
        for j in range(1, block):
            update = update + columns[j] * rows[j]
        held = held - update
        for j in range(block):
            held = jnp.where(index == p + j, rows[j], held)
    return held[:, size:]


def kernel(stages, devs, total, lengths_hbm, forces_hbm, weights_hbm, order_hbm, operators_ref,
           solution_ref, residual_ref,
           lengths_ref, forces_ref, weights_ref, order_ref, ops, pick, start, search, image, remainder, scaled, second, following, product, applied,
           fwd_src, fwd_dst, fwdlow_src, fwdlow_dst, right_src, right_dst, ret_src, ret_dst, retlow_src, retlow_dst,
           ret2_src, ret2_dst, sums_src, sums_dst, last_src, last_dst,
           ops_sem, small_sem, halo_send, halo_recv, sums_send, sums_recv, last_send, last_recv):
    number, loads, breadth = forces_ref.shape
    grp, dev = lax.axis_index("grp"), lax.axis_index("dev")
    me = grp * devs + dev
    has_prev, has_next = me > 0, me < total - 1
    before, after = jnp.maximum(me - 1, 0), jnp.minimum(me + 1, total - 1)
    prev_id = (lax.div(before, devs), lax.rem(before, devs))
    next_id = (lax.div(after, devs), lax.rem(after, devs))

    barrier = pltpu.get_barrier_semaphore()
    partners = 0
    for stage in stages:
        for offset in range(1, stage[0]):
            pl.semaphore_signal(barrier, inc=1, device_id=peer(stage, offset, grp, dev, devs), device_id_type=MESH)
            partners += 1

    @pl.when(has_prev)
    def _():
        pl.semaphore_signal(barrier, inc=1, device_id=prev_id, device_id_type=MESH)

    @pl.when(has_next)
    def _():
        pl.semaphore_signal(barrier, inc=1, device_id=next_id, device_id_type=MESH)

    fetching = [
        pltpu.make_async_copy(source, target, small_sem.at[i])
        for i, (source, target) in enumerate((
            (order_hbm, order_ref), (forces_hbm, forces_ref), (weights_hbm, weights_ref), (lengths_hbm, lengths_ref),
        ))
    ]
    for copy in fetching:
        copy.start()
    loading = [pltpu.make_async_copy(operators_ref.at[l], ops.at[l], ops_sem.at[l]) for l in reversed(range(number))]
    for copy in loading:
        copy.start()

    def remote(slot, source, target, where):
        return pltpu.make_async_remote_copy(
            src_ref=source, dst_ref=target, send_sem=halo_send.at[slot], recv_sem=halo_recv.at[slot],
            device_id=where, device_id_type=MESH,
        )

    forward = remote(0, fwd_src, fwd_dst, next_id)
    forward_low = remote(1, fwdlow_src, fwdlow_dst, next_id)
    forward_right = remote(2, right_src, right_dst, next_id)
    back = remote(3, ret_src, ret_dst, prev_id)
    back_low = remote(4, retlow_src, retlow_dst, prev_id)
    back_second = remote(5, ret2_src, ret2_dst, prev_id)

    def start_if(condition, *copies):
        @pl.when(condition)
        def _():
            for copy in copies:
                copy.start()

    def arrived(condition, copy, buffer):
        @pl.when(condition)
        def _():
            copy.wait_recv()

        @pl.when(jnp.logical_not(condition))
        def _():
            buffer[...] = jnp.zeros_like(buffer)

    for copy in fetching:
        copy.wait()
    positions = lax.broadcasted_iota(jnp.int32, (1, breadth), 1)
    masks = []
    for l in range(number):
        k = me * number + l
        live = jnp.where(k < total * number - 1, lengths_ref[k], 0)
        masks.append(positions < live)
    slots = lax.broadcasted_iota(jnp.int32, (breadth, breadth), 0)

    last = number - 1
    turned = [None] * number
    stacks = [None] * number
    for l in reversed(range(number)):
        pick[l] = jnp.where(slots == order_ref[l : l + 1, :], 1.0, 0.0).astype(BF16)
        start[l] = jnp.where(masks[l], forces_ref[l], 0.0)
        search[l] = start[l] * weights_ref[l : l + 1, :]
        stacks[l] = jnp.concatenate(split(search[l]), axis=0)
        if l == last:
            spread = [jnp.broadcast_to(x, (16, breadth)) for x in split(weights_ref[l : l + 1, :])]
            sent = dot(jnp.concatenate([stacks[l]] + spread, axis=0), pick[l]).astype(BF16)
            fwd_src[...] = sent[:loads]
            fwdlow_src[...] = sent[loads:]
            pl.semaphore_wait(barrier, partners + has_prev.astype(jnp.int32) + has_next.astype(jnp.int32))
            start_if(has_next, forward, forward_low)
        else:
            turned[l] = dot(stacks[l], pick[l]).astype(BF16)

    def gather(l, field):
        both = dot_nt(jnp.concatenate(split(field), axis=0), pick[l])
        return both[:loads] + both[loads:]

    def apply(l, fields, target):
        target[l] = dot(jnp.concatenate(fields, axis=1), ops[l])

    loading[0].wait()
    joined = jnp.concatenate([turned[last - 1], stacks[last]], axis=1)
    product[last, :, breadth:] = dot(joined, ops[last, :, breadth:])
    both = dot(jnp.concatenate(split(product[last, :loads, breadth:]), axis=0), pick[last])
    right_src[...] = both[:loads] + both[loads:]
    start_if(has_next, forward_right)
    product[last, :, :breadth] = dot(joined, ops[last, :, :breadth])
    for copy in loading[1:]:
        copy.wait()
    for l in range(1, last):
        apply(l, [turned[l - 1], stacks[l]], product)
    product[0] = dot(stacks[0], ops[0, breadth:, :])
    def whole(pair):
        return pair[:loads].astype(F32) + pair[loads:].astype(F32)

    projection = curvature = 0.0
    for l in range(number):
        projection = projection + dot_nt(search[l], start[l], EXACT)
        if l > 0:
            curvature = curvature + dot_nt(search[l], product[l, :loads, breadth:], EXACT)
            curvature = curvature + dot_nt(whole(turned[l - 1]), product[l, :loads, :breadth], EXACT)

    def finish_image(l, left):
        image[l] = jnp.where(masks[l], product[l, :loads, breadth:] + gather(l, left), 0.0)
        scaled[l] = weights_ref[l : l + 1, :] * image[l]
        stacks[l] = jnp.concatenate(split(scaled[l]), axis=0)

    def exchange(s, source, inbox, send_sem, recv_sem):
        copies = []
        for offset in range(1, stages[s][0]):
            place = sum(stage[0] - 1 for stage in stages[:s]) + offset - 1
            copies.append(pltpu.make_async_remote_copy(
                src_ref=source.at[s], dst_ref=inbox.at[place], send_sem=send_sem.at[place],
                recv_sem=recv_sem.at[place], device_id=peer(stages[s], offset, grp, dev, devs),
                device_id_type=MESH,
            ))
            copies[-1].start()
        return copies

    def collect(s, copies, source, inbox):
        first = sum(stage[0] - 1 for stage in stages[:s])
        value = source[s]
        for i, copy in enumerate(copies):
            copy.wait_recv()
            value = value + inbox[first + i]
        return value

    arrived(has_prev, forward, fwd_dst)
    owed = product[0, :loads, :breadth] + dot(fwd_dst[...], ops[0, :breadth, :breadth])
    ret_src[...] = owed
    start_if(has_prev, back)
    product[0, :loads, breadth:] += dot(fwd_dst[...], ops[0, :breadth, breadth:])
    arrived(has_prev, forward_low, fwdlow_dst)
    curvature = curvature + dot_nt(search[0], product[0, :loads, breadth:], EXACT)
    curvature = curvature + dot_nt(
        fwd_dst[...].astype(F32) + fwdlow_dst[:loads].astype(F32), owed, EXACT
    )
    tall = pack(curvature).shape[0]
    sums_src[0] = jnp.concatenate([pack(curvature), pack(projection)], axis=0)
    pending = [exchange(0, sums_src, sums_dst, sums_send, sums_recv)]

    middle = 0.0
    for l in range(last):
        finish_image(l, product[l + 1, :loads, :breadth])
        turned[l] = dot(stacks[l], pick[l]).astype(BF16)
        middle = middle + dot_nt(scaled[l], image[l], EXACT)

    arrived(has_prev, forward_right, right_dst)
    incoming = positions < jnp.where(has_prev, lengths_ref[jnp.maximum(me * number - 1, 0)], 0)
    across = jnp.where(incoming, right_dst[...] + owed, 0.0)
    turned_weights = (
        fwdlow_dst[loads : loads + 16].astype(F32) + fwdlow_dst[loads + 16 : loads + 32].astype(F32)
    )[:1]
    across_scaled = turned_weights * across
    across_stack = jnp.concatenate(split(across_scaled), axis=0)
    middle = middle + dot_nt(across_scaled, across, EXACT)

    def energy(pair, values):
        return dot_nt(whole(pair), values[:loads] + values[loads:], EXACT)

    apply(0, [across_stack, stacks[0]], applied)
    ret2_src[...] = applied[0, :loads, :breadth] + applied[0, loads:, :breadth]
    outer = energy(across_stack, applied[0, :, :breadth]) + energy(stacks[0], applied[0, :, breadth:])
    for l in range(1, last):
        apply(l, [turned[l - 1], stacks[l]], applied)
        outer = outer + energy(turned[l - 1], applied[l, :, :breadth]) + energy(stacks[l], applied[l, :, breadth:])
    applied[last] = dot(turned[last - 1], ops[last, :breadth, :])
    outer = outer + energy(turned[last - 1], applied[last, :, :breadth])

    for s in range(1, len(stages)):
        sums_src[s] = collect(s - 1, pending[-1], sums_src, sums_dst)
        pending.append(exchange(s, sums_src, sums_dst, sums_send, sums_recv))

    arrived(has_next, back, ret_dst)
    finish_image(last, ret_dst[...])
    own = dot(stacks[last], ops[last, breadth:, breadth:])
    outer = outer + energy(stacks[last], own + 2.0 * applied[last, :, breadth:])
    last_src[0] = jnp.concatenate([pack(middle), pack(outer)], axis=0)
    trailing = [exchange(0, last_src, last_dst, last_send, last_recv)]
    start_if(has_prev, back_second)

    product[0, loads:, :] += dot(fwdlow_dst[:loads], ops[0, :breadth, :])
    retlow_src[...] = product[0, loads:, :breadth].astype(BF16)
    start_if(has_prev, back_low)
    applied[last, :, breadth:] += own
    applied[last, :, :breadth] += dot(stacks[last], ops[last, breadth:, :breadth])

    def advance():
        for s in range(1, len(stages)):
            last_src[s] = collect(s - 1, trailing[-1], last_src, last_dst)
            trailing.append(exchange(s, last_src, last_dst, last_send, last_recv))

    summed = collect(len(stages) - 1, pending[-1], sums_src, sums_dst)
    curvature = unpack(summed[:tall], loads)
    projection = unpack(summed[tall:], loads)
    identity = jnp.where(
        lax.broadcasted_iota(jnp.int32, (loads, loads), 0) == lax.broadcasted_iota(jnp.int32, (loads, loads), 1), 1.0, 0.0
    )
    solved = eliminate(curvature, jnp.concatenate([projection, identity], axis=1), advance)
    alpha, inverse = solved[:, :loads], solved[:, loads:]
    for l in range(number):
        right = applied[l, :loads, breadth:] + applied[l, loads:, breadth:]
        if l < last:
            left_low = product[l + 1, loads:, :breadth].astype(BF16)
            left = applied[l + 1, :loads, :breadth] + applied[l + 1, loads:, :breadth]
        else:
            arrived(has_next, back_low, retlow_dst)
            left_low = retlow_dst[...]
            arrived(has_next, back_second, ret2_dst)
            left = ret2_dst[...]
        remainder[l] = jnp.where(masks[l], product[l, loads:, breadth:] + dot_nt(left_low, pick[l]), 0.0)
        second[l] = jnp.where(masks[l], right + gather(l, left), 0.0)
    for l in range(number):
        solution_ref[l] = small_tn(alpha, search[l])
        residual_ref[l] = start[l] - small_tn(alpha, image[l])
        following[l] = small_tn(alpha, scaled[l])
        second[l] = small_tn(alpha, second[l])
        image[l] += remainder[l]
    summed = collect(len(stages) - 1, trailing[-1], last_src, last_dst)
    middle, outer = unpack(summed[:tall], loads), unpack(summed[tall:], loads)
    outer = 0.5 * (outer + outer.T)
    carried = small(middle, alpha)
    shift = small(inverse, carried)
    again = small_tn(alpha, small(outer, alpha) - small(middle, shift))
    alpha2 = eliminate(again, small_tn(alpha, carried - curvature))
    for l in range(number):
        solution_ref[l] += small_tn(alpha2, small_tn(shift, search[l]) - following[l])
        residual_ref[l] -= small_tn(alpha2, small_tn(shift, image[l]) - second[l])

    @pl.when(has_next)
    def _():
        for copy in (forward, forward_low, forward_right):
            copy.wait_send()

    @pl.when(has_prev)
    def _():
        for copy in (back, back_low, back_second):
            copy.wait_send()

    for copies in pending + trailing:
        for copy in copies:
            copy.wait_send()


def hand_over(*fields):
    count, number = len(fields), fields[0].shape[0]

    def copies(*refs):
        sources, targets = refs[:count], refs[count : 2 * count]
        held, in_sems, out_sems = refs[2 * count :]
        places = [(i, l) for i in range(count) for l in range(number)]
        inward = [
            pltpu.make_async_copy(sources[i].at[l], held.at[n], in_sems.at[n]) for n, (i, l) in enumerate(places)
        ]
        outward = [
            pltpu.make_async_copy(held.at[n], targets[i].at[l], out_sems.at[n]) for n, (i, l) in enumerate(places)
        ]
        for copy in inward:
            copy.start()
        for arriving, leaving in zip(inward, outward):
            arriving.wait()
            leaving.start()
        for copy in outward:
            copy.wait()

    anywhere = pl.BlockSpec(memory_space=pl.ANY)
    return tuple(pl.pallas_call(
        copies,
        out_shape=[jax.ShapeDtypeStruct(field.shape, field.dtype) for field in fields],
        in_specs=[anywhere] * count,
        out_specs=[anywhere] * count,
        scratch_shapes=[
            pltpu.VMEM((count * number,) + fields[0].shape[1:], fields[0].dtype),
            pltpu.SemaphoreType.DMA((count * number,)),
            pltpu.SemaphoreType.DMA((count * number,)),
        ],
        compiler_params=pltpu.CompilerParams(vmem_limit_bytes=VMEM_BYTES),
    )(*fields))


def body(stages, devs, total, operators, forces, weights, lengths, slot_order):
    number, loads, breadth = forces.shape
    tall, wide = jax.eval_shape(pack, jax.ShapeDtypeStruct((loads, loads), F32)).shape
    boxes = sum(stage[0] - 1 for stage in stages)
    field = pltpu.VMEM(forces.shape, F32)
    vmem = pl.BlockSpec(memory_space=pltpu.VMEM)
    results = pl.pallas_call(
        functools.partial(kernel, stages, devs, total),
        out_shape=[jax.ShapeDtypeStruct(forces.shape, F32)] * 2,
        in_specs=[pl.BlockSpec(memory_space=pl.ANY)] * 5,
        out_specs=[vmem, vmem],
        scratch_shapes=[
            pltpu.SMEM(lengths.shape, jnp.int32),
            field,
            pltpu.VMEM(weights.shape, F32),
            pltpu.VMEM(slot_order.shape, jnp.int32),
            pltpu.VMEM(operators.shape, BF16),
            pltpu.VMEM((number, breadth, breadth), BF16),
            field, field, field, field, field, field, field,
            pltpu.VMEM((number, 2 * loads, 2 * breadth), F32),
            pltpu.VMEM((number, 2 * loads, 2 * breadth), F32),
            pltpu.VMEM((loads, breadth), BF16),
            pltpu.VMEM((loads, breadth), BF16),
            pltpu.VMEM((loads + 32, breadth), BF16),
            pltpu.VMEM((loads + 32, breadth), BF16),
            pltpu.VMEM((loads, breadth), F32),
            pltpu.VMEM((loads, breadth), F32),
            pltpu.VMEM((loads, breadth), F32),
            pltpu.VMEM((loads, breadth), F32),
            pltpu.VMEM((loads, breadth), BF16),
            pltpu.VMEM((loads, breadth), BF16),
            pltpu.VMEM((loads, breadth), F32),
            pltpu.VMEM((loads, breadth), F32),
            pltpu.VMEM((len(stages), 2 * tall, wide), F32),
            pltpu.VMEM((boxes, 2 * tall, wide), F32),
            pltpu.VMEM((len(stages), 2 * tall, wide), F32),
            pltpu.VMEM((boxes, 2 * tall, wide), F32),
            pltpu.SemaphoreType.DMA((number,)),
            pltpu.SemaphoreType.DMA((4,)),
            pltpu.SemaphoreType.DMA((6,)),
            pltpu.SemaphoreType.DMA((6,)),
            pltpu.SemaphoreType.DMA((boxes,)),
            pltpu.SemaphoreType.DMA((boxes,)),
            pltpu.SemaphoreType.DMA((boxes,)),
            pltpu.SemaphoreType.DMA((boxes,)),
        ],
        compiler_params=pltpu.CompilerParams(
            collective_id=0, has_side_effects=True, vmem_limit_bytes=VMEM_BYTES
        ),
        cost_estimate=pl.CostEstimate(
            flops=12 * number * loads * 4 * breadth * breadth,
            bytes_accessed=operators.size * 2 + 4 * forces.size * 4,
            transcendentals=0,
        ),
    )(lengths, forces, weights, slot_order, operators)
    return hand_over(*results)


def solution(mesh):
    devs, groups = mesh.shape["dev"], mesh.shape["grp"]
    stages = plan_stages(groups, devs)
    in_specs = (
        P(("grp", "dev"), None, None),
        P(("grp", "dev"), None, None),
        P(("grp", "dev"), None),
        P(),
        P(("grp", "dev"), None),
    )
    out_specs = (P(("grp", "dev"), None, None), P(("grp", "dev"), None, None))
    return jax.shard_map(
        functools.partial(body, stages, devs, devs * groups),
        mesh=mesh, in_specs=in_specs, out_specs=out_specs, check_vma=False,
    )
```

```python
import functools

import jax
import jax.numpy as jnp
from jax import lax
from jax.experimental import pallas as pl
from jax.experimental.pallas import tpu as pltpu
from jax.sharding import PartitionSpec as P

MESH = pl.DeviceIdType.MESH
F32, BF16 = jnp.float32, jnp.bfloat16
VMEM_BYTES = 60 * 1024 * 1024
EXACT = lax.Precision.HIGHEST


def plan_stages(groups, devs):
    factors = []
    while groups > 1:
        factor = next((f for f in (4, 3, 2, 5, 7) if groups % f == 0), groups)
        factors.append(factor)
        groups //= factor
    first = factors[0] if factors else 1
    stages, stride = [(devs * first, None, first)], first
    for factor in factors[1:]:
        stages.append((factor, stride, factor))
        stride *= factor
    return [stage for stage in stages if stage[0] > 1]


def peer(stage, offset, grp, dev, devs):
    size, stride, factor = stage
    if stride is None:
        low = lax.rem(grp, factor)
        place = lax.rem(low * devs + dev + offset, size)
        return grp - low + lax.div(place, devs), lax.rem(place, devs)
    digit = lax.rem(lax.div(grp, stride), factor)
    return grp + (lax.rem(digit + offset, factor) - digit) * stride, dev


def split(x):
    high = x.astype(BF16)
    return high, (x - high.astype(F32)).astype(BF16)


def dot(x, y):
    return jnp.dot(x, y, preferred_element_type=F32)


def dot_nt(x, y, precision=None):
    return lax.dot_general(
        x, y, (((1,), (1,)), ((), ())), precision=precision, preferred_element_type=F32
    )


def small(x, y):
    return jnp.dot(x, y, precision=EXACT, preferred_element_type=F32)


def small_tn(x, y):
    return lax.dot_general(
        x, y, (((0,), (0,)), ((), ())), precision=EXACT, preferred_element_type=F32
    )


def pair(x):
    return jnp.concatenate(split(x), axis=0)


def cross(first, second):
    size = first.shape[0] // 2
    four = dot_nt(first, second)
    both = four[:size] + four[size:]
    return both[:, :size] + both[:, size:]


def mix(matrix, field):
    high, low = split(matrix)
    field_high, field_low = split(field)
    return lax.dot_general(
        jnp.concatenate([high, low, high], axis=0),
        jnp.concatenate([field_high, field_high, field_low], axis=0),
        (((0,), (0,)), ((), ())), preferred_element_type=F32,
    )


def pack(matrix):
    size = matrix.shape[0]
    parts = max(1, min(128 // size, size // 8))
    rows = size // parts
    return jnp.concatenate([matrix[i * rows : (i + 1) * rows] for i in range(parts)], axis=1)


def unpack(packed, size):
    parts = packed.shape[1] // size
    return jnp.concatenate([packed[:, i * size : (i + 1) * size] for i in range(parts)], axis=0)


def eliminate(matrix, targets, between=None):
    size = matrix.shape[0]
    held = jnp.concatenate([matrix, targets], axis=1)
    width = held.shape[1]
    index = lax.broadcasted_iota(jnp.int32, (size, 1), 0)
    block = 4 if size % 4 == 0 else 1
    for p in range(0, size, block):
        if between is not None and p == size // 2:
            between()
        rows = [held[p + i : p + i + 1, :] for i in range(block)]
        entries = [
            [jnp.broadcast_to(row[:, p + j : p + j + 1], (1, width)) for j in range(block)] for row in rows
        ]
        columns = [held[:, p + j : p + j + 1] for j in range(block)]
        for i in range(block):
            scale = 1.0 / entries[i][i]
            rows[i] = rows[i] * scale
            entries[i] = [entry * scale for entry in entries[i]]
            for k in range(block):
                if k != i:
                    factor = entries[k][i]
                    rows[k] = rows[k] - factor * rows[i]
                    entries[k] = [a - factor * b for a, b in zip(entries[k], entries[i])]
        update = columns[0] * rows[0]
        for j in range(1, block):
            update = update + columns[j] * rows[j]
        held = held - update
        for j in range(block):
            held = jnp.where(index == p + j, rows[j], held)
    return held[:, size:]


def kernel(stages, devs, total, lengths_hbm, forces_hbm, weights_hbm, order_hbm, operators_ref,
           solution_ref, residual_ref,
           lengths_ref, forces_ref, weights_ref, order_ref, ops, pick, start, search, image, remainder, scaled, second, following, base, product, applied,
           fwd_src, fwd_dst, fwdlow_src, fwdlow_dst, right_src, right_dst, ret_src, ret_dst, retlow_src, retlow_dst,
           ret2_src, ret2_dst, sums_src, sums_dst, last_src, last_dst,
           ops_sem, small_sem, out_sem, halo_send, halo_recv, sums_send, sums_recv, last_send, last_recv):
    number, loads, breadth = forces_ref.shape
    grp, dev = lax.axis_index("grp"), lax.axis_index("dev")
    me = grp * devs + dev
    has_prev, has_next = me > 0, me < total - 1
    before, after = jnp.maximum(me - 1, 0), jnp.minimum(me + 1, total - 1)
    prev_id = (lax.div(before, devs), lax.rem(before, devs))
    next_id = (lax.div(after, devs), lax.rem(after, devs))

    barrier = pltpu.get_barrier_semaphore()
    partners = 0
    for stage in stages:
        for offset in range(1, stage[0]):
            pl.semaphore_signal(barrier, inc=1, device_id=peer(stage, offset, grp, dev, devs), device_id_type=MESH)
            partners += 1

    @pl.when(has_prev)
    def _():
        pl.semaphore_signal(barrier, inc=1, device_id=prev_id, device_id_type=MESH)

    @pl.when(has_next)
    def _():
        pl.semaphore_signal(barrier, inc=1, device_id=next_id, device_id_type=MESH)

    fetching = [
        pltpu.make_async_copy(source, target, small_sem.at[i])
        for i, (source, target) in enumerate((
            (order_hbm, order_ref), (forces_hbm, forces_ref), (weights_hbm, weights_ref), (lengths_hbm, lengths_ref),
        ))
    ]
    for copy in fetching:
        copy.start()
    loading = [pltpu.make_async_copy(operators_ref.at[l], ops.at[l], ops_sem.at[l]) for l in reversed(range(number))]
    for copy in loading:
        copy.start()

    def remote(slot, source, target, where):
        return pltpu.make_async_remote_copy(
            src_ref=source, dst_ref=target, send_sem=halo_send.at[slot], recv_sem=halo_recv.at[slot],
            device_id=where, device_id_type=MESH,
        )

    forward = remote(0, fwd_src, fwd_dst, next_id)
    forward_low = remote(1, fwdlow_src, fwdlow_dst, next_id)
    forward_right = remote(2, right_src, right_dst, next_id)
    back = remote(3, ret_src, ret_dst, prev_id)
    back_low = remote(4, retlow_src, retlow_dst, prev_id)
    back_second = remote(5, ret2_src, ret2_dst, prev_id)

    def start_if(condition, *copies):
        @pl.when(condition)
        def _():
            for copy in copies:
                copy.start()

    def arrived(condition, copy, buffer):
        @pl.when(condition)
        def _():
            copy.wait_recv()

        @pl.when(jnp.logical_not(condition))
        def _():
            buffer[...] = jnp.zeros_like(buffer)

    for copy in fetching:
        copy.wait()
    positions = lax.broadcasted_iota(jnp.int32, (1, breadth), 1)
    masks = []
    for l in range(number):
        k = me * number + l
        live = jnp.where(k < total * number - 1, lengths_ref[k], 0)
        masks.append(positions < live)
    slots = lax.broadcasted_iota(jnp.int32, (breadth, breadth), 0)

    last = number - 1
    turned = [None] * number
    stacks = [None] * number
    for l in reversed(range(number)):
        pick[l] = jnp.where(slots == order_ref[l : l + 1, :], 1.0, 0.0).astype(BF16)
        start[l] = jnp.where(masks[l], forces_ref[l], 0.0)
        search[l] = start[l] * weights_ref[l : l + 1, :]
        stacks[l] = jnp.concatenate(split(search[l]), axis=0)
        if l == last:
            spread = [jnp.broadcast_to(x, (16, breadth)) for x in split(weights_ref[l : l + 1, :])]
            sent = dot(jnp.concatenate([stacks[l]] + spread, axis=0), pick[l]).astype(BF16)
            fwd_src[...] = sent[:loads]
            fwdlow_src[...] = sent[loads:]
            pl.semaphore_wait(barrier, partners + has_prev.astype(jnp.int32) + has_next.astype(jnp.int32))
            start_if(has_next, forward, forward_low)
        else:
            turned[l] = dot(stacks[l], pick[l]).astype(BF16)

    def gather(l, field):
        both = dot_nt(jnp.concatenate(split(field), axis=0), pick[l])
        return both[:loads] + both[loads:]

    def apply(l, fields, target):
        target[l] = dot(jnp.concatenate(fields, axis=1), ops[l])

    loading[0].wait()
    joined = jnp.concatenate([turned[last - 1], stacks[last]], axis=1)
    product[last, :, breadth:] = dot(joined, ops[last, :, breadth:])
    both = dot(jnp.concatenate(split(product[last, :loads, breadth:]), axis=0), pick[last])
    right_src[...] = both[:loads] + both[loads:]
    start_if(has_next, forward_right)
    product[last, :, :breadth] = dot(joined, ops[last, :, :breadth])
    for copy in loading[1:]:
        copy.wait()
    for l in range(1, last):
        apply(l, [turned[l - 1], stacks[l]], product)
    product[0] = dot(stacks[0], ops[0, breadth:, :])
    projection = curvature = 0.0
    for l in range(number):
        projection = projection + cross(stacks[l], pair(start[l]))
        if l > 0:
            curvature = curvature + cross(
                jnp.concatenate([turned[l - 1], stacks[l]], axis=1), pair(product[l, :loads, :])
            )

    def finish_image(l, left):
        image[l] = jnp.where(masks[l], product[l, :loads, breadth:] + gather(l, left), 0.0)
        scaled[l] = weights_ref[l : l + 1, :] * image[l]
        stacks[l] = jnp.concatenate(split(scaled[l]), axis=0)

    def exchange(s, source, inbox, send_sem, recv_sem):
        copies = []
        for offset in range(1, stages[s][0]):
            place = sum(stage[0] - 1 for stage in stages[:s]) + offset - 1
            copies.append(pltpu.make_async_remote_copy(
                src_ref=source.at[s], dst_ref=inbox.at[place], send_sem=send_sem.at[place],
                recv_sem=recv_sem.at[place], device_id=peer(stages[s], offset, grp, dev, devs),
                device_id_type=MESH,
            ))
            copies[-1].start()
        return copies

    def collect(s, copies, source, inbox):
        first = sum(stage[0] - 1 for stage in stages[:s])
        value = source[s]
        for i, copy in enumerate(copies):
            copy.wait_recv()
            value = value + inbox[first + i]
        return value

    arrived(has_prev, forward, fwd_dst)
    owed = product[0, :loads, :breadth] + dot(fwd_dst[...], ops[0, :breadth, :breadth])
    ret_src[...] = owed
    start_if(has_prev, back)
    product[0, :loads, breadth:] += dot(fwd_dst[...], ops[0, :breadth, breadth:])
    arrived(has_prev, forward_low, fwdlow_dst)
    arriving = jnp.concatenate([fwd_dst[...], fwdlow_dst[:loads]], axis=0)
    curvature = curvature + cross(arriving, pair(owed)) + cross(stacks[0], pair(product[0, :loads, breadth:]))
    tall = pack(curvature).shape[0]
    sums_src[0] = jnp.concatenate([pack(curvature), pack(projection)], axis=0)
    pending = [exchange(0, sums_src, sums_dst, sums_send, sums_recv)]

    middle = 0.0
    for l in range(last):
        finish_image(l, product[l + 1, :loads, :breadth])
        turned[l] = dot(stacks[l], pick[l]).astype(BF16)
        middle = middle + cross(stacks[l], pair(image[l]))

    arrived(has_prev, forward_right, right_dst)
    incoming = positions < jnp.where(has_prev, lengths_ref[jnp.maximum(me * number - 1, 0)], 0)
    across = jnp.where(incoming, right_dst[...] + owed, 0.0)
    turned_weights = (
        fwdlow_dst[loads : loads + 16].astype(F32) + fwdlow_dst[loads + 16 : loads + 32].astype(F32)
    )[:1]
    across_scaled = turned_weights * across
    across_stack = jnp.concatenate(split(across_scaled), axis=0)
    middle = middle + cross(across_stack, pair(across))

    def energy(field, values):
        return cross(field, pair(values[:loads] + values[loads:]))

    apply(0, [across_stack, stacks[0]], applied)
    ret2_src[...] = applied[0, :loads, :breadth] + applied[0, loads:, :breadth]
    outer = energy(across_stack, applied[0, :, :breadth]) + energy(stacks[0], applied[0, :, breadth:])
    for l in range(1, last):
        apply(l, [turned[l - 1], stacks[l]], applied)
        outer = outer + energy(turned[l - 1], applied[l, :, :breadth]) + energy(stacks[l], applied[l, :, breadth:])
    applied[last] = dot(turned[last - 1], ops[last, :breadth, :])
    outer = outer + energy(turned[last - 1], applied[last, :, :breadth])

    for s in range(1, len(stages)):
        sums_src[s] = collect(s - 1, pending[-1], sums_src, sums_dst)
        pending.append(exchange(s, sums_src, sums_dst, sums_send, sums_recv))

    arrived(has_next, back, ret_dst)
    finish_image(last, ret_dst[...])
    own = dot(stacks[last], ops[last, breadth:, breadth:])
    outer = outer + energy(stacks[last], own + 2.0 * applied[last, :, breadth:])
    last_src[0] = jnp.concatenate([pack(middle), pack(outer)], axis=0)
    trailing = [exchange(0, last_src, last_dst, last_send, last_recv)]
    start_if(has_prev, back_second)

    product[0, loads:, :] += dot(fwdlow_dst[:loads], ops[0, :breadth, :])
    retlow_src[...] = product[0, loads:, :breadth].astype(BF16)
    start_if(has_prev, back_low)
    applied[last, :, breadth:] += own
    applied[last, :, :breadth] += dot(stacks[last], ops[last, breadth:, :breadth])

    def advance():
        for s in range(1, len(stages)):
            last_src[s] = collect(s - 1, trailing[-1], last_src, last_dst)
            trailing.append(exchange(s, last_src, last_dst, last_send, last_recv))

    summed = collect(len(stages) - 1, pending[-1], sums_src, sums_dst)
    curvature = unpack(summed[:tall], loads)
    projection = unpack(summed[tall:], loads)
    identity = jnp.where(
        lax.broadcasted_iota(jnp.int32, (loads, loads), 0) == lax.broadcasted_iota(jnp.int32, (loads, loads), 1), 1.0, 0.0
    )
    solved = eliminate(curvature, jnp.concatenate([projection, identity], axis=1), advance)
    alpha, inverse = solved[:, :loads], solved[:, loads:]
    for l in range(number):
        right = applied[l, :loads, breadth:] + applied[l, loads:, breadth:]
        if l < last:
            left_low = product[l + 1, loads:, :breadth].astype(BF16)
            left = applied[l + 1, :loads, :breadth] + applied[l + 1, loads:, :breadth]
        else:
            arrived(has_next, back_low, retlow_dst)
            left_low = retlow_dst[...]
            arrived(has_next, back_second, ret2_dst)
            left = ret2_dst[...]
        remainder[l] = jnp.where(masks[l], product[l, loads:, breadth:] + dot_nt(left_low, pick[l]), 0.0)
        second[l] = jnp.where(masks[l], right + gather(l, left), 0.0)
    for l in range(number):
        base[0, l] = mix(alpha, search[l])
        base[1, l] = start[l] - mix(alpha, image[l])
        following[l] = mix(alpha, scaled[l])
        second[l] = mix(alpha, second[l])
        image[l] += remainder[l]
    summed = collect(len(stages) - 1, trailing[-1], last_src, last_dst)
    middle, outer = unpack(summed[:tall], loads), unpack(summed[tall:], loads)
    outer = 0.5 * (outer + outer.T)
    carried = small(middle, alpha)
    shift = small(inverse, carried)
    again = small_tn(alpha, small(outer, alpha) - small(middle, shift))
    alpha2 = eliminate(again, small_tn(alpha, carried - curvature))
    leaving = []
    for l in range(number):
        base[0, l] += mix(alpha2, mix(shift, search[l]) - following[l])
        leaving.append(pltpu.make_async_copy(base.at[0, l], solution_ref.at[l], out_sem.at[0, l]))
        leaving[-1].start()
    for l in range(number):
        base[1, l] -= mix(alpha2, mix(shift, image[l]) - second[l])
        leaving.append(pltpu.make_async_copy(base.at[1, l], residual_ref.at[l], out_sem.at[1, l]))
        leaving[-1].start()

    @pl.when(has_next)
    def _():
        for copy in (forward, forward_low, forward_right):
            copy.wait_send()

    @pl.when(has_prev)
    def _():
        for copy in (back, back_low, back_second):
            copy.wait_send()

    for copy in leaving:
        copy.wait()
    for copies in pending + trailing:
        for copy in copies:
            copy.wait_send()


def hand_over(*fields):
    count, number = len(fields), fields[0].shape[0]

    def copies(*refs):
        sources, targets = refs[:count], refs[count : 2 * count]
        held, in_sems, out_sems = refs[2 * count :]
        places = [(i, l) for i in range(count) for l in range(number)]
        inward = [
            pltpu.make_async_copy(sources[i].at[l], held.at[n], in_sems.at[n]) for n, (i, l) in enumerate(places)
        ]
        outward = [
            pltpu.make_async_copy(held.at[n], targets[i].at[l], out_sems.at[n]) for n, (i, l) in enumerate(places)
        ]
        for copy in inward:
            copy.start()
        for arriving, leaving in zip(inward, outward):
            arriving.wait()
            leaving.start()
        for copy in outward:
            copy.wait()

    anywhere = pl.BlockSpec(memory_space=pl.ANY)
    return tuple(pl.pallas_call(
        copies,
        out_shape=[jax.ShapeDtypeStruct(field.shape, field.dtype) for field in fields],
        in_specs=[anywhere] * count,
        out_specs=[anywhere] * count,
        scratch_shapes=[
            pltpu.VMEM((count * number,) + fields[0].shape[1:], fields[0].dtype),
            pltpu.SemaphoreType.DMA((count * number,)),
            pltpu.SemaphoreType.DMA((count * number,)),
        ],
        compiler_params=pltpu.CompilerParams(vmem_limit_bytes=VMEM_BYTES),
    )(*fields))


def body(stages, devs, total, operators, forces, weights, lengths, slot_order):
    number, loads, breadth = forces.shape
    tall, wide = jax.eval_shape(pack, jax.ShapeDtypeStruct((loads, loads), F32)).shape
    boxes = sum(stage[0] - 1 for stage in stages)
    field = pltpu.VMEM(forces.shape, F32)
    results = pl.pallas_call(
        functools.partial(kernel, stages, devs, total),
        out_shape=[jax.ShapeDtypeStruct(forces.shape, F32)] * 2,
        in_specs=[pl.BlockSpec(memory_space=pl.ANY)] * 5,
        out_specs=[pl.BlockSpec(memory_space=pl.ANY)] * 2,
        scratch_shapes=[
            pltpu.SMEM(lengths.shape, jnp.int32),
            field,
            pltpu.VMEM(weights.shape, F32),
            pltpu.VMEM(slot_order.shape, jnp.int32),
            pltpu.VMEM(operators.shape, BF16),
            pltpu.VMEM((number, breadth, breadth), BF16),
            field, field, field, field, field, field, field,
            pltpu.VMEM((2,) + forces.shape, F32),
            pltpu.VMEM((number, 2 * loads, 2 * breadth), F32),
            pltpu.VMEM((number, 2 * loads, 2 * breadth), F32),
            pltpu.VMEM((loads, breadth), BF16),
            pltpu.VMEM((loads, breadth), BF16),
            pltpu.VMEM((loads + 32, breadth), BF16),
            pltpu.VMEM((loads + 32, breadth), BF16),
            pltpu.VMEM((loads, breadth), F32),
            pltpu.VMEM((loads, breadth), F32),
            pltpu.VMEM((loads, breadth), F32),
            pltpu.VMEM((loads, breadth), F32),
            pltpu.VMEM((loads, breadth), BF16),
            pltpu.VMEM((loads, breadth), BF16),
            pltpu.VMEM((loads, breadth), F32),
            pltpu.VMEM((loads, breadth), F32),
            pltpu.VMEM((len(stages), 2 * tall, wide), F32),
            pltpu.VMEM((boxes, 2 * tall, wide), F32),
            pltpu.VMEM((len(stages), 2 * tall, wide), F32),
            pltpu.VMEM((boxes, 2 * tall, wide), F32),
            pltpu.SemaphoreType.DMA((number,)),
            pltpu.SemaphoreType.DMA((4,)),
            pltpu.SemaphoreType.DMA((2, number)),
            pltpu.SemaphoreType.DMA((6,)),
            pltpu.SemaphoreType.DMA((6,)),
            pltpu.SemaphoreType.DMA((boxes,)),
            pltpu.SemaphoreType.DMA((boxes,)),
            pltpu.SemaphoreType.DMA((boxes,)),
            pltpu.SemaphoreType.DMA((boxes,)),
        ],
        compiler_params=pltpu.CompilerParams(
            collective_id=0, has_side_effects=True, vmem_limit_bytes=VMEM_BYTES
        ),
        cost_estimate=pl.CostEstimate(
            flops=12 * number * loads * 4 * breadth * breadth,
            bytes_accessed=operators.size * 2 + 4 * forces.size * 4,
            transcendentals=0,
        ),
    )(lengths, forces, weights, slot_order, operators)
    return hand_over(*results)


def solution(mesh):
    devs, groups = mesh.shape["dev"], mesh.shape["grp"]
    stages = plan_stages(groups, devs)
    in_specs = (
        P(("grp", "dev"), None, None),
        P(("grp", "dev"), None, None),
        P(("grp", "dev"), None),
        P(),
        P(("grp", "dev"), None),
    )
    out_specs = (P(("grp", "dev"), None, None), P(("grp", "dev"), None, None))
    return jax.shard_map(
        functools.partial(body, stages, devs, devs * groups),
        mesh=mesh, in_specs=in_specs, out_specs=out_specs, check_vma=False,
    )
```

```python
import functools

import jax
import jax.numpy as jnp
from jax import lax
from jax.experimental import pallas as pl
from jax.experimental.pallas import tpu as pltpu
from jax.sharding import PartitionSpec as P

MESH = pl.DeviceIdType.MESH
F32, BF16 = jnp.float32, jnp.bfloat16
VMEM_BYTES = 60 * 1024 * 1024
EXACT = lax.Precision.HIGHEST


def plan_stages(groups, devs):
    factors = []
    while groups > 1:
        factor = next((f for f in (4, 3, 2, 5, 7) if groups % f == 0), groups)
        factors.append(factor)
        groups //= factor
    first = factors[0] if factors else 1
    stages, stride = [(devs * first, None, first)], first
    for factor in factors[1:]:
        stages.append((factor, stride, factor))
        stride *= factor
    return [stage for stage in stages if stage[0] > 1]


def peer(stage, offset, grp, dev, devs):
    size, stride, factor = stage
    if stride is None:
        low = lax.rem(grp, factor)
        place = lax.rem(low * devs + dev + offset, size)
        return grp - low + lax.div(place, devs), lax.rem(place, devs)
    digit = lax.rem(lax.div(grp, stride), factor)
    return grp + (lax.rem(digit + offset, factor) - digit) * stride, dev


def split(x):
    high = x.astype(BF16)
    return high, (x - high.astype(F32)).astype(BF16)


def dot(x, y):
    return jnp.dot(x, y, preferred_element_type=F32)


def dot_nt(x, y, precision=None):
    return lax.dot_general(
        x, y, (((1,), (1,)), ((), ())), precision=precision, preferred_element_type=F32
    )


def small(x, y):
    return jnp.dot(x, y, precision=EXACT, preferred_element_type=F32)


def small_tn(x, y):
    return lax.dot_general(
        x, y, (((0,), (0,)), ((), ())), precision=EXACT, preferred_element_type=F32
    )


def pair(x):
    return jnp.concatenate(split(x), axis=0)


def cross(first, second):
    size = first.shape[0] // 2
    four = dot_nt(first, second)
    both = four[:size] + four[size:]
    return both[:, :size] + both[:, size:]


def mix(matrix, field):
    high, low = split(matrix)
    field_high, field_low = split(field)
    return lax.dot_general(
        jnp.concatenate([high, low, high], axis=0),
        jnp.concatenate([field_high, field_high, field_low], axis=0),
        (((0,), (0,)), ((), ())), preferred_element_type=F32,
    )


def pack(matrix):
    size = matrix.shape[0]
    parts = max(1, min(128 // size, size // 8))
    rows = size // parts
    return jnp.concatenate([matrix[i * rows : (i + 1) * rows] for i in range(parts)], axis=1)


def unpack(packed, size):
    parts = packed.shape[1] // size
    return jnp.concatenate([packed[:, i * size : (i + 1) * size] for i in range(parts)], axis=0)


def eliminate(matrix, targets, between=None):
    size = matrix.shape[0]
    held = jnp.concatenate([matrix, targets], axis=1)
    width = held.shape[1]
    index = lax.broadcasted_iota(jnp.int32, (size, 1), 0)
    block = 4 if size % 4 == 0 else 1
    for p in range(0, size, block):
        if between is not None and p == size // 2:
            between()
        rows = [held[p + i : p + i + 1, :] for i in range(block)]
        entries = [
            [jnp.broadcast_to(row[:, p + j : p + j + 1], (1, width)) for j in range(block)] for row in rows
        ]
        columns = [held[:, p + j : p + j + 1] for j in range(block)]
        for i in range(block):
            scale = 1.0 / entries[i][i]
            rows[i] = rows[i] * scale
            entries[i] = [entry * scale for entry in entries[i]]
            for k in range(block):
                if k != i:
                    factor = entries[k][i]
                    rows[k] = rows[k] - factor * rows[i]
                    entries[k] = [a - factor * b for a, b in zip(entries[k], entries[i])]
        update = columns[0] * rows[0]
        for j in range(1, block):
            update = update + columns[j] * rows[j]
        held = held - update
        for j in range(block):
            held = jnp.where(index == p + j, rows[j], held)
    return held[:, size:]


def kernel(stages, devs, total, lengths_hbm, forces_hbm, weights_hbm, order_hbm, operators_ref,
           solution_ref, residual_ref,
           lengths_ref, forces_ref, weights_ref, order_ref, ops, pick, start, search, image, remainder, scaled, second, following, base, product, applied,
           fwd_src, fwd_dst, fwdlow_src, fwdlow_dst, right_src, right_dst, ret_src, ret_dst, retlow_src, retlow_dst,
           ret2_src, ret2_dst, sums_src, sums_dst, mid_src, mid_dst, last_src, last_dst,
           ops_sem, small_sem, out_sem, halo_send, halo_recv, sums_send, sums_recv, mid_send, mid_recv, last_send, last_recv):
    number, loads, breadth = forces_ref.shape
    grp, dev = lax.axis_index("grp"), lax.axis_index("dev")
    me = grp * devs + dev
    has_prev, has_next = me > 0, me < total - 1
    before, after = jnp.maximum(me - 1, 0), jnp.minimum(me + 1, total - 1)
    prev_id = (lax.div(before, devs), lax.rem(before, devs))
    next_id = (lax.div(after, devs), lax.rem(after, devs))

    barrier = pltpu.get_barrier_semaphore()
    partners = 0
    for stage in stages:
        for offset in range(1, stage[0]):
            pl.semaphore_signal(barrier, inc=1, device_id=peer(stage, offset, grp, dev, devs), device_id_type=MESH)
            partners += 1

    @pl.when(has_prev)
    def _():
        pl.semaphore_signal(barrier, inc=1, device_id=prev_id, device_id_type=MESH)

    @pl.when(has_next)
    def _():
        pl.semaphore_signal(barrier, inc=1, device_id=next_id, device_id_type=MESH)

    fetching = [
        pltpu.make_async_copy(source, target, small_sem.at[i])
        for i, (source, target) in enumerate((
            (order_hbm, order_ref), (forces_hbm, forces_ref), (weights_hbm, weights_ref), (lengths_hbm, lengths_ref),
        ))
    ]
    for copy in fetching:
        copy.start()
    loading = [pltpu.make_async_copy(operators_ref.at[l], ops.at[l], ops_sem.at[l]) for l in reversed(range(number))]
    for copy in loading:
        copy.start()

    def remote(slot, source, target, where):
        return pltpu.make_async_remote_copy(
            src_ref=source, dst_ref=target, send_sem=halo_send.at[slot], recv_sem=halo_recv.at[slot],
            device_id=where, device_id_type=MESH,
        )

    forward = remote(0, fwd_src, fwd_dst, next_id)
    forward_low = remote(1, fwdlow_src, fwdlow_dst, next_id)
    forward_right = remote(2, right_src, right_dst, next_id)
    back = remote(3, ret_src, ret_dst, prev_id)
    back_low = remote(4, retlow_src, retlow_dst, prev_id)
    back_second = remote(5, ret2_src, ret2_dst, prev_id)

    def start_if(condition, *copies):
        @pl.when(condition)
        def _():
            for copy in copies:
                copy.start()

    def arrived(condition, copy, buffer):
        @pl.when(condition)
        def _():
            copy.wait_recv()

        @pl.when(jnp.logical_not(condition))
        def _():
            buffer[...] = jnp.zeros_like(buffer)

    for copy in fetching:
        copy.wait()
    positions = lax.broadcasted_iota(jnp.int32, (1, breadth), 1)
    masks = []
    for l in range(number):
        k = me * number + l
        live = jnp.where(k < total * number - 1, lengths_ref[k], 0)
        masks.append(positions < live)
    slots = lax.broadcasted_iota(jnp.int32, (breadth, breadth), 0)

    last = number - 1
    turned = [None] * number
    stacks = [None] * number
    for l in reversed(range(number)):
        pick[l] = jnp.where(slots == order_ref[l : l + 1, :], 1.0, 0.0).astype(BF16)
        start[l] = jnp.where(masks[l], forces_ref[l], 0.0)
        search[l] = start[l] * weights_ref[l : l + 1, :]
        stacks[l] = jnp.concatenate(split(search[l]), axis=0)
        if l == last:
            spread = [jnp.broadcast_to(x, (16, breadth)) for x in split(weights_ref[l : l + 1, :])]
            sent = dot(jnp.concatenate([stacks[l]] + spread, axis=0), pick[l]).astype(BF16)
            fwd_src[...] = sent[:loads]
            fwdlow_src[...] = sent[loads:]
            pl.semaphore_wait(barrier, partners + has_prev.astype(jnp.int32) + has_next.astype(jnp.int32))
            start_if(has_next, forward, forward_low)
        else:
            turned[l] = dot(stacks[l], pick[l]).astype(BF16)

    def gather(l, field):
        both = dot_nt(jnp.concatenate(split(field), axis=0), pick[l])
        return both[:loads] + both[loads:]

    def apply(l, fields, target):
        target[l] = dot(jnp.concatenate(fields, axis=1), ops[l])

    loading[0].wait()
    joined = jnp.concatenate([turned[last - 1], stacks[last]], axis=1)
    product[last, :, breadth:] = dot(joined, ops[last, :, breadth:])
    both = dot(jnp.concatenate(split(product[last, :loads, breadth:]), axis=0), pick[last])
    right_src[...] = both[:loads] + both[loads:]
    start_if(has_next, forward_right)
    product[last, :, :breadth] = dot(joined, ops[last, :, :breadth])
    for copy in loading[1:]:
        copy.wait()
    for l in range(1, last):
        apply(l, [turned[l - 1], stacks[l]], product)
    product[0] = dot(stacks[0], ops[0, breadth:, :])
    projection = curvature = 0.0
    for l in range(number):
        projection = projection + cross(stacks[l], pair(start[l]))
        if l > 0:
            curvature = curvature + cross(
                jnp.concatenate([turned[l - 1], stacks[l]], axis=1), pair(product[l, :loads, :])
            )

    def finish_image(l, left):
        image[l] = jnp.where(masks[l], product[l, :loads, breadth:] + gather(l, left), 0.0)
        scaled[l] = weights_ref[l : l + 1, :] * image[l]
        stacks[l] = jnp.concatenate(split(scaled[l]), axis=0)

    def exchange(s, source, inbox, send_sem, recv_sem):
        copies = []
        for offset in range(1, stages[s][0]):
            place = sum(stage[0] - 1 for stage in stages[:s]) + offset - 1
            copies.append(pltpu.make_async_remote_copy(
                src_ref=source.at[s], dst_ref=inbox.at[place], send_sem=send_sem.at[place],
                recv_sem=recv_sem.at[place], device_id=peer(stages[s], offset, grp, dev, devs),
                device_id_type=MESH,
            ))
            copies[-1].start()
        return copies

    def collect(s, copies, source, inbox):
        first = sum(stage[0] - 1 for stage in stages[:s])
        value = source[s]
        for i, copy in enumerate(copies):
            copy.wait_recv()
            value = value + inbox[first + i]
        return value

    arrived(has_prev, forward, fwd_dst)
    owed = product[0, :loads, :breadth] + dot(fwd_dst[...], ops[0, :breadth, :breadth])
    ret_src[...] = owed
    start_if(has_prev, back)
    product[0, :loads, breadth:] += dot(fwd_dst[...], ops[0, :breadth, breadth:])
    arrived(has_prev, forward_low, fwdlow_dst)
    arriving = jnp.concatenate([fwd_dst[...], fwdlow_dst[:loads]], axis=0)
    curvature = curvature + cross(arriving, pair(owed)) + cross(stacks[0], pair(product[0, :loads, breadth:]))
    tall = pack(curvature).shape[0]
    sums_src[0] = jnp.concatenate([pack(curvature), pack(projection)], axis=0)
    pending = [exchange(0, sums_src, sums_dst, sums_send, sums_recv)]

    middle = 0.0
    for l in range(last):
        finish_image(l, product[l + 1, :loads, :breadth])
        turned[l] = dot(stacks[l], pick[l]).astype(BF16)
        middle = middle + cross(stacks[l], pair(image[l]))

    arrived(has_prev, forward_right, right_dst)
    incoming = positions < jnp.where(has_prev, lengths_ref[jnp.maximum(me * number - 1, 0)], 0)
    across = jnp.where(incoming, right_dst[...] + owed, 0.0)
    turned_weights = (
        fwdlow_dst[loads : loads + 16].astype(F32) + fwdlow_dst[loads + 16 : loads + 32].astype(F32)
    )[:1]
    across_scaled = turned_weights * across
    across_stack = jnp.concatenate(split(across_scaled), axis=0)
    middle = middle + cross(across_stack, pair(across))
    mid_src[0] = pack(middle)
    between = [exchange(0, mid_src, mid_dst, mid_send, mid_recv)]

    def energy(field, values):
        return cross(field, pair(values[:loads] + values[loads:]))

    apply(0, [across_stack, stacks[0]], applied)
    ret2_src[...] = applied[0, :loads, :breadth] + applied[0, loads:, :breadth]
    outer = energy(across_stack, applied[0, :, :breadth]) + energy(stacks[0], applied[0, :, breadth:])
    for l in range(1, last):
        apply(l, [turned[l - 1], stacks[l]], applied)
        outer = outer + energy(turned[l - 1], applied[l, :, :breadth]) + energy(stacks[l], applied[l, :, breadth:])
    applied[last] = dot(turned[last - 1], ops[last, :breadth, :])
    outer = outer + energy(turned[last - 1], applied[last, :, :breadth])

    for s in range(1, len(stages)):
        sums_src[s] = collect(s - 1, pending[-1], sums_src, sums_dst)
        pending.append(exchange(s, sums_src, sums_dst, sums_send, sums_recv))
        mid_src[s] = collect(s - 1, between[-1], mid_src, mid_dst)
        between.append(exchange(s, mid_src, mid_dst, mid_send, mid_recv))

    arrived(has_next, back, ret_dst)
    finish_image(last, ret_dst[...])
    own = dot(stacks[last], ops[last, breadth:, breadth:])
    outer = outer + energy(stacks[last], own + 2.0 * applied[last, :, breadth:])
    last_src[0] = pack(outer)
    trailing = [exchange(0, last_src, last_dst, last_send, last_recv)]
    start_if(has_prev, back_second)

    product[0, loads:, :] += dot(fwdlow_dst[:loads], ops[0, :breadth, :])
    retlow_src[...] = product[0, loads:, :breadth].astype(BF16)
    start_if(has_prev, back_low)
    applied[last, :, breadth:] += own
    applied[last, :, :breadth] += dot(stacks[last], ops[last, breadth:, :breadth])

    def advance():
        for s in range(1, len(stages)):
            last_src[s] = collect(s - 1, trailing[-1], last_src, last_dst)
            trailing.append(exchange(s, last_src, last_dst, last_send, last_recv))

    summed = collect(len(stages) - 1, pending[-1], sums_src, sums_dst)
    curvature = unpack(summed[:tall], loads)
    projection = unpack(summed[tall:], loads)
    identity = jnp.where(
        lax.broadcasted_iota(jnp.int32, (loads, loads), 0) == lax.broadcasted_iota(jnp.int32, (loads, loads), 1), 1.0, 0.0
    )
    solved = eliminate(curvature, jnp.concatenate([projection, identity], axis=1), advance)
    alpha, inverse = solved[:, :loads], solved[:, loads:]
    for l in range(number):
        right = applied[l, :loads, breadth:] + applied[l, loads:, breadth:]
        if l < last:
            left_low = product[l + 1, loads:, :breadth].astype(BF16)
            left = applied[l + 1, :loads, :breadth] + applied[l + 1, loads:, :breadth]
        else:
            arrived(has_next, back_low, retlow_dst)
            left_low = retlow_dst[...]
            arrived(has_next, back_second, ret2_dst)
            left = ret2_dst[...]
        remainder[l] = jnp.where(masks[l], product[l, loads:, breadth:] + dot_nt(left_low, pick[l]), 0.0)
        second[l] = jnp.where(masks[l], right + gather(l, left), 0.0)
    middle = unpack(collect(len(stages) - 1, between[-1], mid_src, mid_dst), loads)
    carried = small(middle, alpha)
    shift = small(inverse, carried)
    known = small(middle, shift)
    right_side = small_tn(alpha, carried - curvature)
    for l in range(number):
        base[0, l] = mix(alpha, search[l])
        base[1, l] = start[l] - mix(alpha, image[l])
        following[l] = mix(shift, search[l]) - mix(alpha, scaled[l])
        second[l] = mix(shift, image[l] + remainder[l]) - mix(alpha, second[l])
    outer = unpack(collect(len(stages) - 1, trailing[-1], last_src, last_dst), loads)
    outer = 0.5 * (outer + outer.T)
    alpha2 = eliminate(small_tn(alpha, small(outer, alpha) - known), right_side)
    leaving = []
    for l in range(number):
        base[0, l] += mix(alpha2, following[l])
        leaving.append(pltpu.make_async_copy(base.at[0, l], solution_ref.at[l], out_sem.at[0, l]))
        leaving[-1].start()
    for l in range(number):
        base[1, l] -= mix(alpha2, second[l])
        leaving.append(pltpu.make_async_copy(base.at[1, l], residual_ref.at[l], out_sem.at[1, l]))
        leaving[-1].start()

    @pl.when(has_next)
    def _():
        for copy in (forward, forward_low, forward_right):
            copy.wait_send()

    @pl.when(has_prev)
    def _():
        for copy in (back, back_low, back_second):
            copy.wait_send()

    for copy in leaving:
        copy.wait()
    for copies in pending + between + trailing:
        for copy in copies:
            copy.wait_send()


def hand_over(*fields):
    count, number = len(fields), fields[0].shape[0]

    def copies(*refs):
        sources, targets = refs[:count], refs[count : 2 * count]
        held, in_sems, out_sems = refs[2 * count :]
        places = [(i, l) for i in range(count) for l in range(number)]
        inward = [
            pltpu.make_async_copy(sources[i].at[l], held.at[n], in_sems.at[n]) for n, (i, l) in enumerate(places)
        ]
        outward = [
            pltpu.make_async_copy(held.at[n], targets[i].at[l], out_sems.at[n]) for n, (i, l) in enumerate(places)
        ]
        for copy in inward:
            copy.start()
        for arriving, leaving in zip(inward, outward):
            arriving.wait()
            leaving.start()
        for copy in outward:
            copy.wait()

    anywhere = pl.BlockSpec(memory_space=pl.ANY)
    return tuple(pl.pallas_call(
        copies,
        out_shape=[jax.ShapeDtypeStruct(field.shape, field.dtype) for field in fields],
        in_specs=[anywhere] * count,
        out_specs=[anywhere] * count,
        scratch_shapes=[
            pltpu.VMEM((count * number,) + fields[0].shape[1:], fields[0].dtype),
            pltpu.SemaphoreType.DMA((count * number,)),
            pltpu.SemaphoreType.DMA((count * number,)),
        ],
        compiler_params=pltpu.CompilerParams(vmem_limit_bytes=VMEM_BYTES),
    )(*fields))


def body(stages, devs, total, operators, forces, weights, lengths, slot_order):
    number, loads, breadth = forces.shape
    tall, wide = jax.eval_shape(pack, jax.ShapeDtypeStruct((loads, loads), F32)).shape
    boxes = sum(stage[0] - 1 for stage in stages)
    field = pltpu.VMEM(forces.shape, F32)
    results = pl.pallas_call(
        functools.partial(kernel, stages, devs, total),
        out_shape=[jax.ShapeDtypeStruct(forces.shape, F32)] * 2,
        in_specs=[pl.BlockSpec(memory_space=pl.ANY)] * 5,
        out_specs=[pl.BlockSpec(memory_space=pl.ANY)] * 2,
        scratch_shapes=[
            pltpu.SMEM(lengths.shape, jnp.int32),
            field,
            pltpu.VMEM(weights.shape, F32),
            pltpu.VMEM(slot_order.shape, jnp.int32),
            pltpu.VMEM(operators.shape, BF16),
            pltpu.VMEM((number, breadth, breadth), BF16),
            field, field, field, field, field, field, field,
            pltpu.VMEM((2,) + forces.shape, F32),
            pltpu.VMEM((number, 2 * loads, 2 * breadth), F32),
            pltpu.VMEM((number, 2 * loads, 2 * breadth), F32),
            pltpu.VMEM((loads, breadth), BF16),
            pltpu.VMEM((loads, breadth), BF16),
            pltpu.VMEM((loads + 32, breadth), BF16),
            pltpu.VMEM((loads + 32, breadth), BF16),
            pltpu.VMEM((loads, breadth), F32),
            pltpu.VMEM((loads, breadth), F32),
            pltpu.VMEM((loads, breadth), F32),
            pltpu.VMEM((loads, breadth), F32),
            pltpu.VMEM((loads, breadth), BF16),
            pltpu.VMEM((loads, breadth), BF16),
            pltpu.VMEM((loads, breadth), F32),
            pltpu.VMEM((loads, breadth), F32),
            pltpu.VMEM((len(stages), 2 * tall, wide), F32),
            pltpu.VMEM((boxes, 2 * tall, wide), F32),
            pltpu.VMEM((len(stages), tall, wide), F32),
            pltpu.VMEM((boxes, tall, wide), F32),
            pltpu.VMEM((len(stages), tall, wide), F32),
            pltpu.VMEM((boxes, tall, wide), F32),
            pltpu.SemaphoreType.DMA((number,)),
            pltpu.SemaphoreType.DMA((4,)),
            pltpu.SemaphoreType.DMA((2, number)),
            pltpu.SemaphoreType.DMA((6,)),
            pltpu.SemaphoreType.DMA((6,)),
            pltpu.SemaphoreType.DMA((boxes,)),
            pltpu.SemaphoreType.DMA((boxes,)),
            pltpu.SemaphoreType.DMA((boxes,)),
            pltpu.SemaphoreType.DMA((boxes,)),
            pltpu.SemaphoreType.DMA((boxes,)),
            pltpu.SemaphoreType.DMA((boxes,)),
        ],
        compiler_params=pltpu.CompilerParams(
            collective_id=0, has_side_effects=True, vmem_limit_bytes=VMEM_BYTES
        ),
        cost_estimate=pl.CostEstimate(
            flops=12 * number * loads * 4 * breadth * breadth,
            bytes_accessed=operators.size * 2 + 4 * forces.size * 4,
            transcendentals=0,
        ),
    )(lengths, forces, weights, slot_order, operators)
    return hand_over(*results)


def solution(mesh):
    devs, groups = mesh.shape["dev"], mesh.shape["grp"]
    stages = plan_stages(groups, devs)
    in_specs = (
        P(("grp", "dev"), None, None),
        P(("grp", "dev"), None, None),
        P(("grp", "dev"), None),
        P(),
        P(("grp", "dev"), None),
    )
    out_specs = (P(("grp", "dev"), None, None), P(("grp", "dev"), None, None))
    return jax.shard_map(
        functools.partial(body, stages, devs, devs * groups),
        mesh=mesh, in_specs=in_specs, out_specs=out_specs, check_vma=False,
    )
```

```python
import functools

import jax
import jax.numpy as jnp
from jax import lax
from jax.experimental import pallas as pl
from jax.experimental.pallas import tpu as pltpu
from jax.sharding import PartitionSpec as P

MESH = pl.DeviceIdType.MESH
F32, BF16 = jnp.float32, jnp.bfloat16
VMEM_BYTES = 60 * 1024 * 1024
EXACT = lax.Precision.HIGHEST


def plan_stages(groups, devs):
    factors = []
    while groups > 1:
        factor = next((f for f in (4, 3, 2, 5, 7) if groups % f == 0), groups)
        factors.append(factor)
        groups //= factor
    first = factors[0] if factors else 1
    stages, stride = [(devs * first, None, first)], first
    for factor in factors[1:]:
        stages.append((factor, stride, factor))
        stride *= factor
    return [stage for stage in stages if stage[0] > 1]


def peer(stage, offset, grp, dev, devs):
    size, stride, factor = stage
    if stride is None:
        low = lax.rem(grp, factor)
        place = lax.rem(low * devs + dev + offset, size)
        return grp - low + lax.div(place, devs), lax.rem(place, devs)
    digit = lax.rem(lax.div(grp, stride), factor)
    return grp + (lax.rem(digit + offset, factor) - digit) * stride, dev


def split(x):
    high = x.astype(BF16)
    return high, (x - high.astype(F32)).astype(BF16)


def dot(x, y):
    return jnp.dot(x, y, preferred_element_type=F32)


def dot_nt(x, y, precision=None):
    return lax.dot_general(
        x, y, (((1,), (1,)), ((), ())), precision=precision, preferred_element_type=F32
    )


def small(x, y):
    return jnp.dot(x, y, precision=EXACT, preferred_element_type=F32)


def small_tn(x, y):
    return lax.dot_general(
        x, y, (((0,), (0,)), ((), ())), precision=EXACT, preferred_element_type=F32
    )


def pair(x):
    return jnp.concatenate(split(x), axis=0)


def cross(first, second):
    size = first.shape[0] // 2
    four = dot_nt(first, second)
    both = four[:size] + four[size:]
    return both[:, :size] + both[:, size:]


def mix(matrix, field):
    high, low = split(matrix)
    field_high, field_low = split(field)
    return lax.dot_general(
        jnp.concatenate([high, low, high], axis=0),
        jnp.concatenate([field_high, field_high, field_low], axis=0),
        (((0,), (0,)), ((), ())), preferred_element_type=F32,
    )


def pack(matrix):
    size = matrix.shape[0]
    parts = max(1, min(128 // size, size // 8))
    rows = size // parts
    return jnp.concatenate([matrix[i * rows : (i + 1) * rows] for i in range(parts)], axis=1)


def unpack(packed, size):
    parts = packed.shape[1] // size
    return jnp.concatenate([packed[:, i * size : (i + 1) * size] for i in range(parts)], axis=0)


def eliminate(matrix, targets, between=None):
    size = matrix.shape[0]
    held = jnp.concatenate([matrix, targets], axis=1)
    width = held.shape[1]
    index = lax.broadcasted_iota(jnp.int32, (size, 1), 0)
    block = 4 if size % 4 == 0 else 1
    for p in range(0, size, block):
        if between is not None and p == size // 2:
            between()
        rows = [held[p + i : p + i + 1, :] for i in range(block)]
        entries = [
            [jnp.broadcast_to(row[:, p + j : p + j + 1], (1, width)) for j in range(block)] for row in rows
        ]
        columns = [held[:, p + j : p + j + 1] for j in range(block)]
        for i in range(block):
            pivot = entries[i][i]
            scale = pl.reciprocal(pivot, approx=True)
            for _ in range(2):
                scale = scale + scale * (1.0 - pivot * scale)
            rows[i] = rows[i] * scale
            entries[i] = [entry * scale for entry in entries[i]]
            for k in range(block):
                if k != i:
                    factor = entries[k][i]
                    rows[k] = rows[k] - factor * rows[i]
                    entries[k] = [a - factor * b for a, b in zip(entries[k], entries[i])]
        update = columns[0] * rows[0]
        for j in range(1, block):
            update = update + columns[j] * rows[j]
        held = held - update
        for j in range(block):
            held = jnp.where(index == p + j, rows[j], held)
    return held[:, size:]


def kernel(stages, devs, total, lengths_hbm, forces_hbm, weights_hbm, order_hbm, operators_ref,
           solution_ref, residual_ref,
           lengths_ref, forces_ref, weights_ref, order_ref, ops, pick, start, search, image, remainder, scaled, second, following, base, product, applied,
           fwd_src, fwd_dst, fwdlow_src, fwdlow_dst, right_src, right_dst, ret_src, ret_dst, retlow_src, retlow_dst,
           ret2_src, ret2_dst, sums_src, sums_dst, mid_src, mid_dst, last_src, last_dst,
           ops_sem, small_sem, out_sem, halo_send, halo_recv, sums_send, sums_recv, mid_send, mid_recv, last_send, last_recv):
    number, loads, breadth = forces_ref.shape
    grp, dev = lax.axis_index("grp"), lax.axis_index("dev")
    me = grp * devs + dev
    has_prev, has_next = me > 0, me < total - 1
    before, after = jnp.maximum(me - 1, 0), jnp.minimum(me + 1, total - 1)
    prev_id = (lax.div(before, devs), lax.rem(before, devs))
    next_id = (lax.div(after, devs), lax.rem(after, devs))

    barrier = pltpu.get_barrier_semaphore()
    partners = 0
    for stage in stages:
        for offset in range(1, stage[0]):
            pl.semaphore_signal(barrier, inc=1, device_id=peer(stage, offset, grp, dev, devs), device_id_type=MESH)
            partners += 1

    @pl.when(has_prev)
    def _():
        pl.semaphore_signal(barrier, inc=1, device_id=prev_id, device_id_type=MESH)

    @pl.when(has_next)
    def _():
        pl.semaphore_signal(barrier, inc=1, device_id=next_id, device_id_type=MESH)

    fetching = [
        pltpu.make_async_copy(source, target, small_sem.at[i])
        for i, (source, target) in enumerate((
            (order_hbm, order_ref), (forces_hbm, forces_ref), (weights_hbm, weights_ref), (lengths_hbm, lengths_ref),
        ))
    ]
    for copy in fetching:
        copy.start()
    loading = [pltpu.make_async_copy(operators_ref.at[l], ops.at[l], ops_sem.at[l]) for l in reversed(range(number))]
    for copy in loading:
        copy.start()

    def remote(slot, source, target, where):
        return pltpu.make_async_remote_copy(
            src_ref=source, dst_ref=target, send_sem=halo_send.at[slot], recv_sem=halo_recv.at[slot],
            device_id=where, device_id_type=MESH,
        )

    forward = remote(0, fwd_src, fwd_dst, next_id)
    forward_low = remote(1, fwdlow_src, fwdlow_dst, next_id)
    forward_right = remote(2, right_src, right_dst, next_id)
    back = remote(3, ret_src, ret_dst, prev_id)
    back_low = remote(4, retlow_src, retlow_dst, prev_id)
    back_second = remote(5, ret2_src, ret2_dst, prev_id)

    def start_if(condition, *copies):
        @pl.when(condition)
        def _():
            for copy in copies:
                copy.start()

    def arrived(condition, copy, buffer):
        @pl.when(condition)
        def _():
            copy.wait_recv()

        @pl.when(jnp.logical_not(condition))
        def _():
            buffer[...] = jnp.zeros_like(buffer)

    for copy in fetching:
        copy.wait()
    positions = lax.broadcasted_iota(jnp.int32, (1, breadth), 1)
    masks = []
    for l in range(number):
        k = me * number + l
        live = jnp.where(k < total * number - 1, lengths_ref[k], 0)
        masks.append(positions < live)
    slots = lax.broadcasted_iota(jnp.int32, (breadth, breadth), 0)

    last = number - 1
    turned = [None] * number
    stacks = [None] * number
    for l in reversed(range(number)):
        pick[l] = jnp.where(slots == order_ref[l : l + 1, :], 1.0, 0.0).astype(BF16)
        start[l] = jnp.where(masks[l], forces_ref[l], 0.0)
        search[l] = start[l] * weights_ref[l : l + 1, :]
        stacks[l] = jnp.concatenate(split(search[l]), axis=0)
        if l == last:
            spread = [jnp.broadcast_to(x, (16, breadth)) for x in split(weights_ref[l : l + 1, :])]
            sent = dot(jnp.concatenate([stacks[l]] + spread, axis=0), pick[l]).astype(BF16)
            fwd_src[...] = sent[:loads]
            fwdlow_src[...] = sent[loads:]
            pl.semaphore_wait(barrier, partners + has_prev.astype(jnp.int32) + has_next.astype(jnp.int32))
            start_if(has_next, forward, forward_low)
        else:
            turned[l] = dot(stacks[l], pick[l]).astype(BF16)

    def gather(l, field):
        both = dot_nt(jnp.concatenate(split(field), axis=0), pick[l])
        return both[:loads] + both[loads:]

    def apply(l, fields, target):
        target[l] = dot(jnp.concatenate(fields, axis=1), ops[l])

    loading[0].wait()
    joined = jnp.concatenate([turned[last - 1], stacks[last]], axis=1)
    product[last, :, breadth:] = dot(joined, ops[last, :, breadth:])
    both = dot(jnp.concatenate(split(product[last, :loads, breadth:]), axis=0), pick[last])
    right_src[...] = both[:loads] + both[loads:]
    start_if(has_next, forward_right)
    product[last, :, :breadth] = dot(joined, ops[last, :, :breadth])
    for copy in loading[1:]:
        copy.wait()
    for l in range(1, last):
        apply(l, [turned[l - 1], stacks[l]], product)
    product[0] = dot(stacks[0], ops[0, breadth:, :])
    projection = curvature = 0.0
    for l in range(number):
        projection = projection + cross(stacks[l], pair(start[l]))
        if l > 0:
            curvature = curvature + cross(
                jnp.concatenate([turned[l - 1], stacks[l]], axis=1), pair(product[l, :loads, :])
            )

    def finish_image(l, left):
        image[l] = jnp.where(masks[l], product[l, :loads, breadth:] + gather(l, left), 0.0)
        scaled[l] = weights_ref[l : l + 1, :] * image[l]
        stacks[l] = jnp.concatenate(split(scaled[l]), axis=0)

    def exchange(s, source, inbox, send_sem, recv_sem):
        copies = []
        for offset in range(1, stages[s][0]):
            place = sum(stage[0] - 1 for stage in stages[:s]) + offset - 1
            copies.append(pltpu.make_async_remote_copy(
                src_ref=source.at[s], dst_ref=inbox.at[place], send_sem=send_sem.at[place],
                recv_sem=recv_sem.at[place], device_id=peer(stages[s], offset, grp, dev, devs),
                device_id_type=MESH,
            ))
            copies[-1].start()
        return copies

    def collect(s, copies, source, inbox):
        first = sum(stage[0] - 1 for stage in stages[:s])
        value = source[s]
        for i, copy in enumerate(copies):
            copy.wait_recv()
            value = value + inbox[first + i]
        return value

    arrived(has_prev, forward, fwd_dst)
    owed = product[0, :loads, :breadth] + dot(fwd_dst[...], ops[0, :breadth, :breadth])
    ret_src[...] = owed
    start_if(has_prev, back)
    product[0, :loads, breadth:] += dot(fwd_dst[...], ops[0, :breadth, breadth:])
    arrived(has_prev, forward_low, fwdlow_dst)
    arriving = jnp.concatenate([fwd_dst[...], fwdlow_dst[:loads]], axis=0)
    curvature = curvature + cross(arriving, pair(owed)) + cross(stacks[0], pair(product[0, :loads, breadth:]))
    tall = pack(curvature).shape[0]
    sums_src[0] = jnp.concatenate([pack(curvature), pack(projection)], axis=0)
    pending = [exchange(0, sums_src, sums_dst, sums_send, sums_recv)]

    middle = 0.0
    for l in range(last):
        finish_image(l, product[l + 1, :loads, :breadth])
        turned[l] = dot(stacks[l], pick[l]).astype(BF16)
        middle = middle + cross(stacks[l], pair(image[l]))

    arrived(has_prev, forward_right, right_dst)
    incoming = positions < jnp.where(has_prev, lengths_ref[jnp.maximum(me * number - 1, 0)], 0)
    across = jnp.where(incoming, right_dst[...] + owed, 0.0)
    turned_weights = (
        fwdlow_dst[loads : loads + 16].astype(F32) + fwdlow_dst[loads + 16 : loads + 32].astype(F32)
    )[:1]
    across_scaled = turned_weights * across
    across_stack = jnp.concatenate(split(across_scaled), axis=0)
    middle = middle + cross(across_stack, pair(across))
    mid_src[0] = pack(middle)
    between = [exchange(0, mid_src, mid_dst, mid_send, mid_recv)]

    def energy(field, values):
        return cross(field, pair(values[:loads] + values[loads:]))

    apply(0, [across_stack, stacks[0]], applied)
    ret2_src[...] = applied[0, :loads, :breadth] + applied[0, loads:, :breadth]
    outer = energy(across_stack, applied[0, :, :breadth]) + energy(stacks[0], applied[0, :, breadth:])
    for l in range(1, last):
        apply(l, [turned[l - 1], stacks[l]], applied)
        outer = outer + energy(turned[l - 1], applied[l, :, :breadth]) + energy(stacks[l], applied[l, :, breadth:])
    applied[last] = dot(turned[last - 1], ops[last, :breadth, :])
    outer = outer + energy(turned[last - 1], applied[last, :, :breadth])

    for s in range(1, len(stages)):
        sums_src[s] = collect(s - 1, pending[-1], sums_src, sums_dst)
        pending.append(exchange(s, sums_src, sums_dst, sums_send, sums_recv))
        mid_src[s] = collect(s - 1, between[-1], mid_src, mid_dst)
        between.append(exchange(s, mid_src, mid_dst, mid_send, mid_recv))

    arrived(has_next, back, ret_dst)
    finish_image(last, ret_dst[...])
    own = dot(stacks[last], ops[last, breadth:, breadth:])
    outer = outer + energy(stacks[last], own + 2.0 * applied[last, :, breadth:])
    last_src[0] = pack(outer)
    trailing = [exchange(0, last_src, last_dst, last_send, last_recv)]
    start_if(has_prev, back_second)

    product[0, loads:, :] += dot(fwdlow_dst[:loads], ops[0, :breadth, :])
    retlow_src[...] = product[0, loads:, :breadth].astype(BF16)
    start_if(has_prev, back_low)
    applied[last, :, breadth:] += own
    applied[last, :, :breadth] += dot(stacks[last], ops[last, breadth:, :breadth])

    def advance():
        for s in range(1, len(stages)):
            last_src[s] = collect(s - 1, trailing[-1], last_src, last_dst)
            trailing.append(exchange(s, last_src, last_dst, last_send, last_recv))

    summed = collect(len(stages) - 1, pending[-1], sums_src, sums_dst)
    curvature = unpack(summed[:tall], loads)
    projection = unpack(summed[tall:], loads)
    identity = jnp.where(
        lax.broadcasted_iota(jnp.int32, (loads, loads), 0) == lax.broadcasted_iota(jnp.int32, (loads, loads), 1), 1.0, 0.0
    )
    solved = eliminate(curvature, jnp.concatenate([projection, identity], axis=1), advance)
    alpha, inverse = solved[:, :loads], solved[:, loads:]
    middle = unpack(collect(len(stages) - 1, between[-1], mid_src, mid_dst), loads)
    carried = small(middle, alpha)
    shift = small(inverse, carried)
    known = small(middle, shift)
    right_side = small_tn(alpha, carried - curvature)
    arrived(has_next, back_low, retlow_dst)
    arrived(has_next, back_second, ret2_dst)
    outer = unpack(collect(len(stages) - 1, trailing[-1], last_src, last_dst), loads)
    outer = 0.5 * (outer + outer.T)
    alpha2 = eliminate(small_tn(alpha, small(outer, alpha) - known), right_side)
    for l in range(number):
        right = applied[l, :loads, breadth:] + applied[l, loads:, breadth:]
        if l < last:
            left_low = product[l + 1, loads:, :breadth].astype(BF16)
            left = applied[l + 1, :loads, :breadth] + applied[l + 1, loads:, :breadth]
        else:
            left_low = retlow_dst[...]
            left = ret2_dst[...]
        remainder[l] = jnp.where(masks[l], product[l, loads:, breadth:] + dot_nt(left_low, pick[l]), 0.0)
        second[l] = jnp.where(masks[l], right + gather(l, left), 0.0)
    for l in range(number):
        base[0, l] = mix(alpha, search[l])
        base[1, l] = start[l] - mix(alpha, image[l])
        following[l] = mix(shift, search[l]) - mix(alpha, scaled[l])
        second[l] = mix(shift, image[l] + remainder[l]) - mix(alpha, second[l])
    leaving = []
    for l in range(number):
        base[0, l] += mix(alpha2, following[l])
        leaving.append(pltpu.make_async_copy(base.at[0, l], solution_ref.at[l], out_sem.at[0, l]))
        leaving[-1].start()
    for l in range(number):
        base[1, l] -= mix(alpha2, second[l])
        leaving.append(pltpu.make_async_copy(base.at[1, l], residual_ref.at[l], out_sem.at[1, l]))
        leaving[-1].start()

    @pl.when(has_next)
    def _():
        for copy in (forward, forward_low, forward_right):
            copy.wait_send()

    @pl.when(has_prev)
    def _():
        for copy in (back, back_low, back_second):
            copy.wait_send()

    for copy in leaving:
        copy.wait()
    for copies in pending + between + trailing:
        for copy in copies:
            copy.wait_send()


def hand_over(*fields):
    count, number = len(fields), fields[0].shape[0]

    def copies(*refs):
        sources, targets = refs[:count], refs[count : 2 * count]
        held, in_sems, out_sems = refs[2 * count :]
        places = [(i, l) for i in range(count) for l in range(number)]
        inward = [
            pltpu.make_async_copy(sources[i].at[l], held.at[n], in_sems.at[n]) for n, (i, l) in enumerate(places)
        ]
        outward = [
            pltpu.make_async_copy(held.at[n], targets[i].at[l], out_sems.at[n]) for n, (i, l) in enumerate(places)
        ]
        for copy in inward:
            copy.start()
        for arriving, leaving in zip(inward, outward):
            arriving.wait()
            leaving.start()
        for copy in outward:
            copy.wait()

    anywhere = pl.BlockSpec(memory_space=pl.ANY)
    return tuple(pl.pallas_call(
        copies,
        out_shape=[jax.ShapeDtypeStruct(field.shape, field.dtype) for field in fields],
        in_specs=[anywhere] * count,
        out_specs=[anywhere] * count,
        scratch_shapes=[
            pltpu.VMEM((count * number,) + fields[0].shape[1:], fields[0].dtype),
            pltpu.SemaphoreType.DMA((count * number,)),
            pltpu.SemaphoreType.DMA((count * number,)),
        ],
        compiler_params=pltpu.CompilerParams(vmem_limit_bytes=VMEM_BYTES),
    )(*fields))


def body(stages, devs, total, operators, forces, weights, lengths, slot_order):
    number, loads, breadth = forces.shape
    tall, wide = jax.eval_shape(pack, jax.ShapeDtypeStruct((loads, loads), F32)).shape
    boxes = sum(stage[0] - 1 for stage in stages)
    field = pltpu.VMEM(forces.shape, F32)
    results = pl.pallas_call(
        functools.partial(kernel, stages, devs, total),
        out_shape=[jax.ShapeDtypeStruct(forces.shape, F32)] * 2,
        in_specs=[pl.BlockSpec(memory_space=pl.ANY)] * 5,
        out_specs=[pl.BlockSpec(memory_space=pl.ANY)] * 2,
        scratch_shapes=[
            pltpu.SMEM(lengths.shape, jnp.int32),
            field,
            pltpu.VMEM(weights.shape, F32),
            pltpu.VMEM(slot_order.shape, jnp.int32),
            pltpu.VMEM(operators.shape, BF16),
            pltpu.VMEM((number, breadth, breadth), BF16),
            field, field, field, field, field, field, field,
            pltpu.VMEM((2,) + forces.shape, F32),
            pltpu.VMEM((number, 2 * loads, 2 * breadth), F32),
            pltpu.VMEM((number, 2 * loads, 2 * breadth), F32),
            pltpu.VMEM((loads, breadth), BF16),
            pltpu.VMEM((loads, breadth), BF16),
            pltpu.VMEM((loads + 32, breadth), BF16),
            pltpu.VMEM((loads + 32, breadth), BF16),
            pltpu.VMEM((loads, breadth), F32),
            pltpu.VMEM((loads, breadth), F32),
            pltpu.VMEM((loads, breadth), F32),
            pltpu.VMEM((loads, breadth), F32),
            pltpu.VMEM((loads, breadth), BF16),
            pltpu.VMEM((loads, breadth), BF16),
            pltpu.VMEM((loads, breadth), F32),
            pltpu.VMEM((loads, breadth), F32),
            pltpu.VMEM((len(stages), 2 * tall, wide), F32),
            pltpu.VMEM((boxes, 2 * tall, wide), F32),
            pltpu.VMEM((len(stages), tall, wide), F32),
            pltpu.VMEM((boxes, tall, wide), F32),
            pltpu.VMEM((len(stages), tall, wide), F32),
            pltpu.VMEM((boxes, tall, wide), F32),
            pltpu.SemaphoreType.DMA((number,)),
            pltpu.SemaphoreType.DMA((4,)),
            pltpu.SemaphoreType.DMA((2, number)),
            pltpu.SemaphoreType.DMA((6,)),
            pltpu.SemaphoreType.DMA((6,)),
            pltpu.SemaphoreType.DMA((boxes,)),
            pltpu.SemaphoreType.DMA((boxes,)),
            pltpu.SemaphoreType.DMA((boxes,)),
            pltpu.SemaphoreType.DMA((boxes,)),
            pltpu.SemaphoreType.DMA((boxes,)),
            pltpu.SemaphoreType.DMA((boxes,)),
        ],
        compiler_params=pltpu.CompilerParams(
            collective_id=0, has_side_effects=True, vmem_limit_bytes=VMEM_BYTES
        ),
        cost_estimate=pl.CostEstimate(
            flops=12 * number * loads * 4 * breadth * breadth,
            bytes_accessed=operators.size * 2 + 4 * forces.size * 4,
            transcendentals=0,
        ),
    )(lengths, forces, weights, slot_order, operators)
    return hand_over(*results)


def solution(mesh):
    devs, groups = mesh.shape["dev"], mesh.shape["grp"]
    stages = plan_stages(groups, devs)
    in_specs = (
        P(("grp", "dev"), None, None),
        P(("grp", "dev"), None, None),
        P(("grp", "dev"), None),
        P(),
        P(("grp", "dev"), None),
    )
    out_specs = (P(("grp", "dev"), None, None), P(("grp", "dev"), None, None))
    return jax.shard_map(
        functools.partial(body, stages, devs, devs * groups),
        mesh=mesh, in_specs=in_specs, out_specs=out_specs, check_vma=False,
    )
```
